32 devices in a mesh: seg: 4 (over y, x), sec: 8 (over z, core).
Axes of the slice: x: 2, y: 2, z: 4, core: 2. Of those that a mesh axis runs over, the one named last changes fastest.
Arguments:
- psi: bfloat16 [4, 8, 16, 128, 128], P('seg', 'sec'), may hold values from -6 to 6
- env_build: bfloat16 [4, 8, 12, 128, 128], P('seg', 'sec'), may hold values from -0.5 to 0.5
- env_right: bfloat16 [4, 8, 12, 128, 128], P('seg', 'sec'), may hold values from -0.5 to 0.5
- site_left: bfloat16 [12, 12, 4, 4], replicated, may hold values from -0.4375 to 0.4375
- site_right: bfloat16 [12, 12, 4, 4], replicated, may hold values from -0.4375 to 0.4375
- charge: int32 [16], replicated, may hold values from 0 to 7
- rank: int32 [8], P('sec'), may hold values from 64 to 128
Outputs:
- state: bfloat16 [4, 8, 16, 128, 128], P('seg', 'sec')
- energy: float32 [4], P('seg')
- sector_weight: float32 [4, 8], P('seg', 'sec')
The draws below stay inside these ranges and needn't reach their ends.
All inputs are finite; a program needn't handle non-finite values.
Results may differ from the reference program's by a relative error of at most 0.012.
Values may be sent and summed in bfloat16 or wider, within the bound.
A program may use at most 128 MiB of HBM per device.

```python
import jax
import jax.numpy as jnp
from jax import lax

B = 128
W = 12
D = 4
ITERS = 2
P_SIZE = 16
SECTORS = 8
SEGS = 4


def with_ends(values, rng, low, top_value):
    longest = values.shape.index(max(values.shape))
    spots = []
    for shift in (0, 1):
        where = [jax.random.randint(jax.random.fold_in(rng, axis), (), 0, length) for axis, length in enumerate(values.shape)]
        where[longest] = (where[longest] + shift) % values.shape[longest]
        spots.append(tuple(where))
    return values.at[spots[0]].set(low).at[spots[1]].set(top_value)


def block_scale(own_key, shape, cuts, low, top_value):
    gain = 1.0
    for axis_at, shards_of in cuts:
        heights = jax.random.uniform(jax.random.fold_in(jax.random.fold_in(own_key, 6), axis_at), (shards_of,), jnp.float32, low / len(cuts), top_value / len(cuts))
        gain = gain * jnp.repeat(jnp.exp(heights), shape[axis_at] // shards_of).reshape((-1,) + (1,) * (len(shape) - 1 - axis_at))
    return gain


def bell_draw(own_key, dims, deviation, most, shards=(), dtype=jnp.bfloat16):
    factor_of = block_scale(own_key, dims, shards, -0.22, 0.18) if shards else 1.0
    array = jax.random.normal(own_key, dims, jnp.float32) * deviation * factor_of
    return jnp.minimum(jnp.maximum(array, -most), most).astype(dtype)


def setup_inputs(seed: int = 0) -> dict:
    seeds = jax.random.split(jax.random.key(seed), 8)
    psi = bell_draw(seeds[0], (SEGS, SECTORS, P_SIZE, B, B), 1.0, 6.0, ((0, 4), (1, 8)))
    env_build = bell_draw(seeds[1], (SEGS, SECTORS, W, B, B), B ** -0.5, 0.5, ((0, 4), (1, 8)))
    env_right = bell_draw(seeds[2], (SEGS, SECTORS, W, B, B), B ** -0.5, 0.5, ((0, 4), (1, 8)))
    site_left = bell_draw(seeds[3], (W, W, D, D), (W * D * D) ** -0.5, 0.4375)
    site_right = bell_draw(seeds[4], (W, W, D, D), (W * D * D) ** -0.5, 0.4375)
    charge = with_ends(jax.random.randint(seeds[5], (P_SIZE,), 0, SECTORS), jax.random.fold_in(seeds[5], 1), 0, SECTORS - 1).astype(jnp.int32)
    rank = with_ends(jax.random.randint(seeds[6], (SECTORS,), B // 2, B + 1), jax.random.fold_in(seeds[6], 1), B // 2, B).astype(jnp.int32)
    return {"psi": psi, "env_build": env_build, "env_right": env_right, "site_left": site_left, "site_right": site_right, "charge": charge, "rank": rank}


def pair_mpo(site_left, site_right):
    joined = jnp.einsum('lmxs,mwyt->lwxyst', site_left.astype(jnp.float32), site_right.astype(jnp.float32))
    width = joined.shape[0]
    local = joined.shape[2]
    return joined.reshape(width, width, local * local, local * local).astype(jnp.bfloat16)

def apply_block(x_sector, lenv, renv, mpo, left_row):
    first = jnp.einsum('pab,wbc->pwac', x_sector.astype(jnp.float32), renv.astype(jnp.float32)).astype(jnp.bfloat16)
    third = jnp.einsum('lwqp,pwac->lqac', mpo.astype(jnp.float32), first.astype(jnp.float32)).astype(jnp.bfloat16)
    chosen = jnp.take(lenv, left_row, axis=0)
    return jnp.einsum('qlxa,lqac->qxc', chosen.astype(jnp.float32), third.astype(jnp.float32))

def reference(psi, env_build, env_right, site_left, site_right, charge, rank):
    mpo = pair_mpo(site_left, site_right)
    sectors = psi.shape[1]
    left_of = ((jnp.arange(sectors).astype(jnp.int32)[:, None] - charge[None, :]) % sectors).astype(jnp.int32)
    columns = jnp.arange(B).astype(jnp.int32)
    keep = (columns[None, :] < rank[:, None])[:, None, None, :]
    lin = jnp.concatenate([env_build[:1], env_build[:-1]], axis=0)
    count = float(sectors * P_SIZE * B * B)

    def segment(items):
        psi_seg, lenv, renv = items
        x = psi_seg
        energy = jnp.zeros((), jnp.float32)
        squares = jnp.ones((sectors,), jnp.float32)
        total = jnp.ones((), jnp.float32)
        for step in range(ITERS):
            h = jax.vmap(apply_block, in_axes=(0, None, 0, None, 0))(x, lenv, renv, mpo, left_of)
            xf = x.astype(jnp.float32)
            u = jnp.where(keep, xf - 0.5 * h, 0.0)
            squares = lax.optimization_barrier(jnp.sum(u * u, axis=(1, 2, 3)))
            total = jnp.sum(squares)
            energy = jnp.sum(xf * h) / jnp.sum(xf * xf)
            x = (u * lax.rsqrt(total / count + 1e-06)).astype(jnp.bfloat16)
        return (x, energy, jnp.log(float(sectors) * squares / total))
    state, energy, shares = lax.map(segment, (psi, lin, env_right))
    weight = jnp.cumsum(shares, axis=0)
    return (state, energy, weight)
```

```python
import functools

import jax
import jax.numpy as jnp
from jax import lax
from jax.experimental import pallas as pl
from jax.experimental.pallas import tpu as pltpu
from jax.sharding import PartitionSpec as P

ITERS = 2
CHUNKS = 3
MESH = pl.DeviceIdType.MESH
F32 = jnp.float32
BF16 = jnp.bfloat16


def dot(a, b):
    return jnp.dot(a, b, preferred_element_type=F32)


def iota(shape, dim):
    return lax.broadcasted_iota(jnp.int32, shape, dim)


def onehot(cond):
    return jnp.where(cond, 1.0, 0.0).astype(BF16)


def fold(values):
    return jnp.sum(values.reshape(-1, 8, values.shape[-1]), axis=0)


def whole_sum(tile):
    return jnp.sum(tile, axis=(0, 1), keepdims=True)


def order_block(env_ref, chunk):
    width = env_ref.shape[2]
    per = 8 if chunk < 2 else 4
    first = 0 if chunk < 2 else 8
    cols = 512
    start = chunk * cols if chunk < 2 else 0
    shift = 3 if chunk < 2 else 2
    block = jnp.concatenate([env_ref[first + bond] for bond in range(per)], axis=1)
    row = iota((per * width, cols), 0)
    col = iota((per * width, cols), 1) + start
    place = onehot((row >> 7 == (col & (per - 1))) & ((row & 127) == (col >> shift)))
    return dot(block, place).astype(BF16)


def build_mpo(left_ref, right_ref):
    n = 192
    row = iota((n, 1), 0)
    tail = row >= 128
    q = jnp.where(tail, (row - 128) >> 2, row >> 3)
    bond = jnp.where(tail, 8 + (row & 3), row & 7)
    col = iota((1, n), 1)
    pick = onehot(
        (iota((n, n), 0) >> 4 == iota((n, n), 1) >> 4) & ((iota((n, n), 0) & 3) == (iota((n, n), 1) & 3))
    )
    sixteen = iota((1, 16), 1)
    spread = dot(onehot(bond == sixteen), left_ref[...])
    spread = jnp.where(((col >> 2) & 3) == (q >> 2), spread, 0.0).astype(BF16)
    left = jnp.where(((col >> 2) & 3) == (q & 3), dot(spread, pick), 0.0).astype(BF16)
    spread = dot(onehot((row >> 4) == sixteen), right_ref[...])
    spread = jnp.where(((col >> 2) & 3) == ((row >> 2) & 3), spread, 0.0).astype(BF16)
    right = jnp.where(((col >> 2) & 3) == (row & 3), dot(spread, pick), 0.0).astype(BF16)
    return dot(left, right).astype(BF16)


def kernel(
    nseg, nsec,
    psi_ref, env_ref, renv_ref, left_ref, right_ref, charge_ref, rank_ref,
    state_ref, energy_ref, weight_ref,
    l0, l1, l2, own, x1, x3, mpo, flat, xt, xq, acc, sum_tx, sum_rx, share_tx, share_rx, run,
    shift_sem, up_sem, down_sem, side_sem, recv_sem, sum_send, sum_recv, share_send, share_recv,
):
    seg = lax.axis_index("seg")
    sec = lax.axis_index("sec")
    nz = nsec // 2
    z = sec // 2
    core = sec % 2
    slots = (l0, l1, l2)
    states, width = psi_ref.shape[0], psi_ref.shape[2]

    barrier = pltpu.get_barrier_semaphore()
    for d in range(1, nsec):
        pl.semaphore_signal(barrier, inc=1, device_id=(seg, lax.rem(sec + d, nsec)), device_id_type=MESH)
    for d in range(1, nseg):
        pl.semaphore_signal(barrier, inc=1, device_id=(lax.rem(seg + d, nseg), sec), device_id_type=MESH)

    def copy(src, dst, send, recv, to):
        return pltpu.make_async_remote_copy(
            src_ref=src, dst_ref=dst, send_sem=send, recv_sem=recv, device_id=to, device_id_type=MESH
        )

    def shift(c):
        return copy(own.at[c], slots[c].at[sec], shift_sem.at[c], recv_sem.at[c, sec], (seg + 1, sec))

    def up(c, h):
        s = sec - 2 * h
        return copy(slots[c].at[s], slots[c].at[s], up_sem.at[c, h], recv_sem.at[c, s], (seg, sec + 2))

    def down(c, h):
        s = sec + 2 * h
        return copy(slots[c].at[s], slots[c].at[s], down_sem.at[c, h], recv_sem.at[c, s], (seg, sec - 2))

    def side(c, s):
        return copy(
            slots[c].at[s], slots[c].at[s], side_sem.at[c, s // 2], recv_sem.at[c, s], (seg, sec + 1 - 2 * core)
        )

    def arrived(c, s):
        copy(slots[c].at[s], slots[c].at[s], side_sem.at[c, 0], recv_sem.at[c, s], (seg, sec)).wait_recv()

    def order(c):
        block = order_block(env_ref, c)
        own[c] = block

        @pl.when(seg == 0)
        def _():
            slots[c][sec] = block

    def shift_out(c):
        @pl.when(seg < nseg - 1)
        def _():
            shift(c).start()

    def hop(c, h):
        if h == 0:
            @pl.when(seg > 0)
            def _():
                arrived(c, sec)

            @pl.when(z < nz - 1)
            def _():
                up(c, 0).start()

            @pl.when(z > 0)
            def _():
                down(c, 0).start()

            side(c, sec).start()
            return

        @pl.when(z >= h)
        def _():
            arrived(c, sec - 2 * h)

            @pl.when(z < nz - 1)
            def _():
                up(c, h).start()

            side(c, sec - 2 * h).start()

        @pl.when(z + h < nz)
        def _():
            arrived(c, sec + 2 * h)

            @pl.when(z > 0)
            def _():
                down(c, h).start()

            side(c, sec + 2 * h).start()

    def settle(c):
        for k in range(nz):
            arrived(c, 2 * k + 1 - core)

    def drain():
        for c in range(CHUNKS):
            @pl.when(seg < nseg - 1)
            def _():
                shift(c).wait_send()

            for h in range(nz):
                @pl.when((z >= h) & (z < nz - 1))
                def _():
                    up(c, h).wait_send()

                @pl.when((z + h < nz) & (z > 0))
                def _():
                    down(c, h).wait_send()

                side(c, 2 * h + core).wait_send()

    def flatten(first):
        if first:
            for p in range(states):
                value = psi_ref[p].astype(F32)
                flat[pl.ds(p, width, stride=states), :] = value
        xt[...] = flat[...].astype(BF16)

    def right_apply(w_lo, w_hi):
        def one(w, carry):
            rhs = jnp.concatenate([renv_ref[2 * w], renv_ref[2 * w + 1]], axis=1)
            rows = 512
            for block in range(states * width // rows):
                out = dot(xt[block * rows : (block + 1) * rows, :], rhs).astype(BF16)
                lo = block * rows // states
                for half in range(2):
                    x1[pl.ds(lo, rows // states), pl.ds(pl.multiple_of((2 * w + half) * states, states), states), :] = (
                        out[:, half * width : (half + 1) * width].reshape(rows // states, states, width)
                    )
            return carry

        lax.fori_loop(w_lo, w_hi, one, 0)

    def mpo_apply(lo, hi):
        group = 8
        low = iota((states // 2, 8, width), 1) < 4

        def one(step, carry):
            operator = mpo[...]
            for quad in range(group // 4):
                a = step * group + quad * 4
                tails = []
                for pair in range(2):
                    at = a + 2 * pair
                    rhs = jnp.concatenate([x1[at], x1[at + 1]], axis=1)
                    out = dot(operator, rhs)
                    parts = [out[:, :width], out[:, width:]]
                    heads = [part[:128].reshape(states, 8, width) for part in parts]
                    x3[:, pl.ds(pl.multiple_of(at * 8, 16), 16), :] = jnp.concatenate(heads, axis=1).astype(BF16)
                    a_tail, b_tail = [part[128:].reshape(states // 2, 8, width) for part in parts]
                    even = jnp.where(low, a_tail, pltpu.roll(b_tail, 4, 1))
                    odd = jnp.where(low, pltpu.roll(a_tail, 4, 1), b_tail)
                    tails.append((even, odd))
                even = jnp.concatenate([tails[0][0], tails[1][0]], axis=1).astype(BF16)
                odd = jnp.concatenate([tails[0][1], tails[1][1]], axis=1).astype(BF16)
                both = jnp.stack([even, odd], axis=1).reshape(states, 16, width)
                x3[:, pl.ds(pl.multiple_of(1024 + a * 4, 16), 16), :] = both
            return carry

        lax.fori_loop(lo, hi, one, 0)

    def left_of(q):
        return lax.rem(sec - charge_ref[q] + nsec, nsec)

    keep = iota((width, width), 1) < rank_ref[0]
    per = 4
    zero = jnp.zeros((8, width), F32)

    def left_apply(q, chunks):
        s = left_of(q)
        total = None
        for c in chunks:
            term = dot(slots[c][s], x3[q, c * 512 : (c + 1) * 512, :])
            total = term if total is None else total + term
        return total

    def partial(c):
        def some(step, carry):
            for j in range(per):
                q = step * per + j
                term = left_apply(q, (c,))
                acc[q] = term if c == 0 else acc[q] + term
            return carry

        lax.fori_loop(0, states // per, some, 0)

    def exchange(step):
        for d in range(1, nsec):
            copy(
                sum_tx.at[step], sum_rx.at[step, sec], sum_send.at[step, d], sum_recv.at[step, sec],
                (seg, lax.rem(sec + d, nsec)),
            ).start()

    def collect(step):
        for d in range(1, nsec):
            other = lax.rem(sec + d, nsec)
            copy(
                sum_tx.at[step], sum_rx.at[step, other], sum_send.at[step, d], sum_recv.at[step, other], (seg, other)
            ).wait_recv()
        total = sum_rx[step, 0]
        for other in range(1, nsec):
            total = total + sum_rx[step, other]
        return total

    run[...] = jnp.zeros_like(run)
    order(0)
    pl.semaphore_wait(barrier, nsec + nseg - 2)
    shift_out(0)
    order(1)
    shift_out(1)
    order(2)
    shift_out(2)
    mpo[...] = build_mpo(left_ref, right_ref)
    hop(0, 0)
    flatten(True)
    pairs = renv_ref.shape[0] // 2
    right_apply(0, pairs // 2)
    hop(1, 0)
    right_apply(pairs // 2, pairs)
    hop(2, 0)
    hop(0, 1)
    steps = width // 8
    mpo_apply(0, steps // 2)
    hop(1, 1)
    mpo_apply(steps // 2, steps)
    hop(2, 1)
    for h in range(2, nz):
        for c in range(CHUNKS):
            hop(c, h)
            if h == nz - 1 and c < 2:
                settle(c)
                partial(c)
    settle(2)

    def first(step, squares):
        for j in range(per):
            q = step * per + j
            h = acc[q] + left_apply(q, (2,))
            u = jnp.where(keep, psi_ref[q].astype(F32) - 0.5 * h, 0.0)
            flat[pl.ds(q, width, stride=states), :] = u
            xq[q] = u.astype(BF16)
            squares = squares + fold(u * u)
        return squares

    squares = lax.fori_loop(0, states // per, first, zero)
    sum_tx[0] = jnp.stack([squares, zero, zero])
    sum_rx[0, sec] = jnp.stack([squares, zero, zero])
    exchange(0)
    flatten(False)
    right_apply(0, pairs)
    mpo_apply(0, steps)
    count = float(nsec * states * width * width)
    total = collect(0)
    scale = lax.rsqrt(whole_sum(total[0]) / count + 1e-06)

    def last(step, carry):
        squares, inner, own_sum = carry
        for j in range(per):
            q = step * per + j
            h = left_apply(q, (0, 1, 2)) * scale
            x = xq[q].astype(F32) * scale
            u = jnp.where(keep, x - 0.5 * h, 0.0)
            acc[q] = u
            squares = squares + fold(u * u)
            inner = inner + fold(x * h)
            own_sum = own_sum + fold(x * x)
        return squares, inner, own_sum

    sums = lax.fori_loop(0, states // per, last, (zero, zero, zero))
    sum_tx[1] = jnp.stack(sums)
    sum_rx[1, sec] = jnp.stack(sums)
    exchange(1)
    mine = whole_sum(sums[0])
    total = collect(1)
    all_squares = whole_sum(total[0])
    share = jnp.log(float(nsec) * mine / all_squares)
    share_tx[...] = jnp.broadcast_to(share, share_tx.shape)

    def share_copy(d, back):
        there = seg - d if back else seg + d
        slot = share_rx.at[there if back else seg]
        sem = share_recv.at[there if back else seg]
        return copy(share_tx, slot, share_send.at[d], sem, (there, sec))

    for d in range(1, nseg):
        @pl.when(seg + d < nseg)
        def _():
            share_copy(d, False).start()

    scale = lax.rsqrt(all_squares / count + 1e-06)
    energy_ref[...] = whole_sum(total[1]) / whole_sum(total[2])

    def write(q, carry):
        state_ref[q] = (acc[q] * scale).astype(BF16)
        return carry

    lax.fori_loop(0, states, write, 0)
    run[...] = share_tx[...]
    for d in range(1, nseg):
        @pl.when(seg - d >= 0)
        def _():
            share_copy(d, True).wait_recv()
            run[...] += share_rx[seg - d]

    weight_ref[...] = run[0:1, 0:1]
    drain()
    for step in range(ITERS):
        for d in range(1, nsec):
            copy(
                sum_tx.at[step], sum_rx.at[step, sec], sum_send.at[step, d], sum_recv.at[step, sec],
                (seg, lax.rem(sec + d, nsec)),
            ).wait_send()
    for d in range(1, nseg):
        @pl.when(seg + d < nseg)
        def _():
            share_copy(d, False).wait_send()


def shards(psi, env_build, env_right, site_left, site_right, charge, rank):
    nseg, nsec = lax.axis_size("seg"), lax.axis_size("sec")
    x = psi[0, 0]
    states, width = x.shape[0], x.shape[2]
    bonds = env_build.shape[2]
    left = jnp.pad(site_left.reshape(bonds, -1), ((0, 16 - bonds), (0, 0)))
    right = jnp.pad(site_right.reshape(bonds, -1), ((0, 16 - bonds), (0, 0)))
    vmem = pl.BlockSpec(memory_space=pltpu.VMEM)
    smem = pl.BlockSpec(memory_space=pltpu.SMEM)
    dma = pltpu.SemaphoreType.DMA
    nz = nsec // 2
    slot = pltpu.VMEM((nsec, width, 512), BF16)
    state, energy, weight = pl.pallas_call(
        functools.partial(kernel, nseg, nsec),
        out_shape=(
            jax.ShapeDtypeStruct(x.shape, BF16),
            jax.ShapeDtypeStruct((1, 1), F32),
            jax.ShapeDtypeStruct((1, 1), F32),
        ),
        in_specs=[vmem] * 5 + [smem] * 2,
        out_specs=(vmem, vmem, vmem),
        scratch_shapes=[
            slot, slot, slot,
            pltpu.VMEM((CHUNKS, width, 512), BF16),
            pltpu.VMEM((width, bonds * states, width), BF16),
            pltpu.VMEM((states, bonds * width, width), BF16),
            pltpu.VMEM((bonds * states, bonds * states), BF16),
            pltpu.VMEM((states * width, width), F32),
            pltpu.VMEM((states * width, width), BF16),
            pltpu.VMEM((states, width, width), BF16),
            pltpu.VMEM((states, width, width), F32),
            pltpu.VMEM((ITERS, 3, 8, width), F32),
            pltpu.VMEM((ITERS, nsec, 3, 8, width), F32),
            pltpu.VMEM((8, width), F32),
            pltpu.VMEM((nseg, 8, width), F32),
            pltpu.VMEM((8, width), F32),
            dma((CHUNKS,)),
            dma((CHUNKS, nz)),
            dma((CHUNKS, nz)),
            dma((CHUNKS, nz)),
            dma((CHUNKS, nsec)),
            dma((ITERS, nsec)),
            dma((ITERS, nsec)),
            dma((nseg,)),
            dma((nseg,)),
        ],
        compiler_params=pltpu.CompilerParams(
            collective_id=0, has_side_effects=True, vmem_limit_bytes=52 * 2**20
        ),
    )(x, env_build[0, 0], env_right[0, 0], left, right, charge, rank)
    return (state[None, None], energy.reshape(1), weight.reshape(1, 1))


def solution(mesh):
    return jax.shard_map(
        shards,
        mesh=mesh,
        in_specs=(
            P("seg", "sec", None, None, None),
            P("seg", "sec", None, None, None),
            P("seg", "sec", None, None, None),
            P(),
            P(),
            P(),
            P("sec"),
        ),
        out_specs=(P("seg", "sec", None, None, None), P("seg"), P("seg", "sec")),
        check_vma=False,
    )
```

```python
import functools

import jax
import jax.numpy as jnp
from jax import lax
from jax.experimental import pallas as pl
from jax.experimental.pallas import tpu as pltpu
from jax.sharding import PartitionSpec as P

ITERS = 2
CHUNKS = 4
MESH = pl.DeviceIdType.MESH
F32 = jnp.float32
BF16 = jnp.bfloat16


def dot(a, b):
    return jnp.dot(a, b, preferred_element_type=F32)


def iota(shape, dim):
    return lax.broadcasted_iota(jnp.int32, shape, dim)


def onehot(cond):
    return jnp.where(cond, 1.0, 0.0).astype(BF16)


def fold(values):
    return jnp.sum(values.reshape(-1, 8, values.shape[-1]), axis=0)


def whole_sum(tile):
    return jnp.sum(tile, axis=(0, 1), keepdims=True)


def order_rows(env_ref, lo, rows):
    width = env_ref.shape[2]
    lane = iota((rows, width), 1)
    blocks = []
    for first, per in ((0, 8), (8, 4)):
        parts = [env_ref[first + bond, lo : lo + rows, :].astype(F32) for bond in range(per)]
        for j in range(per):
            block = parts[0] if j == 0 else pltpu.roll(parts[0], width - j, 1)
            for bond in range(1, per):
                turned = parts[bond] if bond == j else pltpu.roll(parts[bond], (bond - j) % width, 1)
                block = jnp.where((lane & (per - 1)) == bond, turned, block)
            blocks.append(block.astype(BF16))
    return blocks


def stage_sites(site_ref, stage):
    stage[...] = jnp.zeros_like(stage)
    local = site_ref.shape[1]
    bonds = site_ref.shape[3]

    def one(bond, carry):
        for new in range(local):
            stage[pl.ds(bond * local * local + new * local, local), 0:bonds] = site_ref[bond, new].astype(F32)
        return carry

    lax.fori_loop(0, site_ref.shape[0], one, 0)


def build_mpo(left_ref, right_ref, stage):
    n = 192
    row = iota((n, 1), 0)
    tail = row >= 128
    q = jnp.where(tail, (row - 128) >> 2, row >> 3)
    bond = jnp.where(tail, 8 + (row & 3), row & 7)
    col = iota((1, n), 1)
    spread = onehot(iota((stage.shape[1], n), 0) == (iota((stage.shape[1], n), 1) >> 4))
    stage_sites(left_ref, stage)
    value = dot(stage[...].astype(BF16), spread)
    value = jnp.where((row & 3) == (col & 3), value, 0.0).astype(BF16)
    value = dot(onehot((bond == (col >> 4)) & ((q >> 2) == ((col >> 2) & 3))), value)
    left = jnp.where((q & 3) == ((col >> 2) & 3), value, 0.0).astype(BF16)
    stage_sites(right_ref, stage)
    value = dot(stage[...].astype(BF16), spread)
    value = jnp.where((row & 3) == (col & 3), value, 0.0).astype(BF16)
    value = dot(onehot(((row >> 4) == (col >> 4)) & (((row >> 2) & 3) == ((col >> 2) & 3))), value)
    right = jnp.where((row & 3) == ((col >> 2) & 3), value, 0.0).astype(BF16)
    return dot(left, right).astype(BF16)


def kernel(
    nseg, nsec,
    psi_hbm, env_hbm, renv_hbm, left_hbm, right_hbm, charge_hbm, rank_hbm,
    state_ref, energy_ref, weight_ref,
    l0, l1, l2, l3, own, psi_ref, env_ref, renv_ref, left_ref, right_ref, charge_ref, rank_ref, x1, x3a, x3b, mpo, stage, flat, xt, xq, acc,
    sum_tx, sum_rx, share_tx, share_rx, run,
    load_sem, shift_sem, up_sem, down_sem, side_sem, recv_sem, sum_send, sum_recv, share_send, share_recv,
):
    seg = lax.axis_index("seg")
    sec = lax.axis_index("sec")
    nz = nsec // 2
    z = sec // 2
    core = sec % 2
    slots = (l0, l1, l2, l3)
    states, width = psi_ref.shape[0], psi_ref.shape[2]
    rows = width // CHUNKS

    pairs = (
        (env_hbm, env_ref), (psi_hbm, psi_ref), (renv_hbm, renv_ref), (left_hbm, left_ref), (right_hbm, right_ref),
        (charge_hbm, charge_ref), (rank_hbm, rank_ref),
    )
    loads = [
        pltpu.make_async_copy(src, dst, load_sem.at[i])
        for i, (src, dst) in enumerate(pairs)
    ]
    for load in loads:
        load.start()

    barrier = pltpu.get_barrier_semaphore()
    for d in range(1, nsec):
        pl.semaphore_signal(barrier, inc=1, device_id=(seg, lax.rem(sec + d, nsec)), device_id_type=MESH)
    for d in range(1, nseg):
        pl.semaphore_signal(barrier, inc=1, device_id=(lax.rem(seg + d, nseg), sec), device_id_type=MESH)

    def copy(src, dst, send, recv, to):
        return pltpu.make_async_remote_copy(
            src_ref=src, dst_ref=dst, send_sem=send, recv_sem=recv, device_id=to, device_id_type=MESH
        )

    def shift(c):
        return copy(own.at[c], slots[c].at[sec], shift_sem.at[c], recv_sem.at[c, sec], (seg + 1, sec))

    def up(c, h):
        s = sec - 2 * h
        return copy(slots[c].at[s], slots[c].at[s], up_sem.at[c, h], recv_sem.at[c, s], (seg, sec + 2))

    def down(c, h):
        s = sec + 2 * h
        return copy(slots[c].at[s], slots[c].at[s], down_sem.at[c, h], recv_sem.at[c, s], (seg, sec - 2))

    def side(c, s):
        return copy(
            slots[c].at[s], slots[c].at[s], side_sem.at[c, s // 2], recv_sem.at[c, s], (seg, sec + 1 - 2 * core)
        )

    def arrived(c, s):
        copy(slots[c].at[s], slots[c].at[s], side_sem.at[c, 0], recv_sem.at[c, s], (seg, sec)).wait_recv()

    def order(c):
        for j, block in enumerate(order_rows(env_ref, c * rows, rows)):
            own[c, :, j * width : (j + 1) * width] = block

        @pl.when(seg == 0)
        def _():
            slots[c][sec] = own[c]

    def shift_out(c):
        @pl.when(seg < nseg - 1)
        def _():
            shift(c).start()

    def hop(c, h):
        if h == 0:
            @pl.when(seg > 0)
            def _():
                arrived(c, sec)

            @pl.when(z < nz - 1)
            def _():
                up(c, 0).start()

            @pl.when(z > 0)
            def _():
                down(c, 0).start()

            side(c, sec).start()
            return

        @pl.when(z >= h)
        def _():
            arrived(c, sec - 2 * h)

            @pl.when(z < nz - 1)
            def _():
                up(c, h).start()

            side(c, sec - 2 * h).start()

        @pl.when(z + h < nz)
        def _():
            arrived(c, sec + 2 * h)

            @pl.when(z > 0)
            def _():
                down(c, h).start()

            side(c, sec + 2 * h).start()

    def settle(c):
        for k in range(nz):
            arrived(c, 2 * k + 1 - core)

    def drain():
        for c in range(CHUNKS):
            @pl.when(seg < nseg - 1)
            def _():
                shift(c).wait_send()

            for h in range(nz):
                @pl.when((z >= h) & (z < nz - 1))
                def _():
                    up(c, h).wait_send()

                @pl.when((z + h < nz) & (z > 0))
                def _():
                    down(c, h).wait_send()

                side(c, 2 * h + core).wait_send()

    def flatten(c):
        for p in range(states):
            flat[pl.ds(p, rows, stride=states), :] = psi_ref[p, c * rows : (c + 1) * rows, :].astype(F32)

    def right_apply():
        xt[...] = flat[...].astype(BF16)

        def one(w, carry):
            rhs = jnp.concatenate([renv_ref[2 * w], renv_ref[2 * w + 1]], axis=1)
            out = dot(xt[...], rhs).astype(BF16)
            for half in range(2):
                x1[:, pl.ds(pl.multiple_of((2 * w + half) * states, states), states), :] = (
                    out[:, half * width : (half + 1) * width].reshape(rows, states, width)
                )
            return carry

        lax.fori_loop(0, renv_ref.shape[0] // 2, one, 0)

    def mpo_apply(c, x3):
        group = 16
        low = iota((states // 2, 8, width), 1) < 4

        def one(step, carry):
            operator = mpo[...]
            a = step * group
            at = pl.multiple_of(c * rows + a, group)

            def pair(j):
                out = dot(operator, jnp.concatenate([x1[a + j], x1[a + j + 8]], axis=1))
                parts = [out[:, :width], out[:, width:]]
                heads = [part[:128].reshape(states, 8, width) for part in parts]
                x3[:, pl.ds(pl.multiple_of(j * width + at, 16), 16), :] = jnp.concatenate(heads, axis=1).astype(BF16)
                return [part[128:].reshape(states // 2, 8, width) for part in parts]

            for j in range(4):
                evens, odds = [], []
                for a_tail, b_tail in zip(pair(j), pair(j + 4)):
                    evens.append(jnp.where(low, a_tail, pltpu.roll(b_tail, 4, 1)))
                    odds.append(jnp.where(low, pltpu.roll(a_tail, 4, 1), b_tail))
                even = jnp.concatenate(evens, axis=1).astype(BF16)
                odd = jnp.concatenate(odds, axis=1).astype(BF16)
                both = jnp.stack([even, odd], axis=1).reshape(states, 16, width)
                x3[:, pl.ds(pl.multiple_of((8 + j) * width + at, 16), 16), :] = both
            return carry

        lax.fori_loop(0, rows // group, one, 0)

    def left_of(q):
        return lax.rem(sec - charge_ref[q] + nsec, nsec)

    per = 4
    zero = jnp.zeros((8, width), F32)

    def first(c, squares, keep):
        def some(step, squares):
            for j in range(per):
                q = step * per + j
                h = dot(slots[c][left_of(q)], x3a[q])
                u = jnp.where(keep, psi_ref[q, c * rows : (c + 1) * rows, :].astype(F32) - 0.5 * h, 0.0)
                flat[pl.ds(q, rows, stride=states), :] = u
                xq[q, c * rows : (c + 1) * rows, :] = u.astype(BF16)
                squares = squares + fold(u * u)
            return squares

        return lax.fori_loop(0, states // per, some, squares)

    def exchange(step):
        for d in range(1, nsec):
            copy(
                sum_tx.at[step], sum_rx.at[step, sec], sum_send.at[step, d], sum_recv.at[step, sec],
                (seg, lax.rem(sec + d, nsec)),
            ).start()

    def collect(step):
        for d in range(1, nsec):
            other = lax.rem(sec + d, nsec)
            copy(
                sum_tx.at[step], sum_rx.at[step, other], sum_send.at[step, d], sum_recv.at[step, other], (seg, other)
            ).wait_recv()
        total = sum_rx[step, 0]
        for other in range(1, nsec):
            total = total + sum_rx[step, other]
        return total

    loads[0].wait()
    order(0)
    pl.semaphore_wait(barrier, nsec + nseg - 2)
    shift_out(0)
    for c in range(1, CHUNKS):
        order(c)
        shift_out(c)
    for load in loads[1:]:
        load.wait()
    mpo[...] = build_mpo(left_ref, right_ref, stage)
    keep = iota((rows, width), 1) < rank_ref[0]
    squares = zero
    for t in range(CHUNKS + nz - 1):
        for c in reversed(range(CHUNKS)):
            if 0 <= t - c < nz:
                hop(c, t - c)
        if t < CHUNKS:
            flatten(t)
            right_apply()
            mpo_apply(t, x3a)
        c = t - nz + 1
        if c >= 0:
            settle(c)
            squares = first(c, squares, keep)
            if c == CHUNKS - 1:
                sums = jnp.stack([squares, zero, zero])
                sum_tx[0] = sums
                sum_rx[0, sec] = sums
                exchange(0)
            right_apply()
            mpo_apply(c, x3b)

    count = float(nsec * states * width * width)
    total = collect(0)
    scale = lax.rsqrt(whole_sum(total[0]) / count + 1e-06)

    keep_all = iota((width, width), 1) < rank_ref[0]

    def last(step, carry):
        squares, inner, own_sum = carry
        for j in range(per):
            q = step * per + j
            s = left_of(q)
            h = dot(jnp.concatenate([slot[s] for slot in slots], axis=0), x3b[q]) * scale
            x = xq[q].astype(F32) * scale
            u = jnp.where(keep_all, x - 0.5 * h, 0.0)
            acc[q] = u
            squares = squares + fold(u * u)
            inner = inner + fold(x * h)
            own_sum = own_sum + fold(x * x)
        return squares, inner, own_sum

    sums = lax.fori_loop(0, states // per, last, (zero, zero, zero))
    sum_tx[1] = jnp.stack(sums)
    sum_rx[1, sec] = jnp.stack(sums)
    exchange(1)
    mine = whole_sum(sums[0])
    total = collect(1)
    all_squares = whole_sum(total[0])
    share = jnp.log(float(nsec) * mine / all_squares)
    share_tx[...] = jnp.broadcast_to(share, share_tx.shape)

    def share_copy(d, back):
        there = seg - d if back else seg + d
        slot = share_rx.at[there if back else seg]
        sem = share_recv.at[there if back else seg]
        return copy(share_tx, slot, share_send.at[d], sem, (there, sec))

    for d in range(1, nseg):
        @pl.when(seg + d < nseg)
        def _():
            share_copy(d, False).start()

    scale = lax.rsqrt(all_squares / count + 1e-06)
    energy_ref[...] = whole_sum(total[1]) / whole_sum(total[2])

    def write(q, carry):
        state_ref[q] = (acc[q] * scale).astype(BF16)
        return carry

    lax.fori_loop(0, states, write, 0)
    run[...] = share_tx[...]
    for d in range(1, nseg):
        @pl.when(seg - d >= 0)
        def _():
            share_copy(d, True).wait_recv()
            run[...] += share_rx[seg - d]

    weight_ref[...] = run[0:1, 0:1]
    drain()
    for step in range(ITERS):
        for d in range(1, nsec):
            copy(
                sum_tx.at[step], sum_rx.at[step, sec], sum_send.at[step, d], sum_recv.at[step, sec],
                (seg, lax.rem(sec + d, nsec)),
            ).wait_send()
    for d in range(1, nseg):
        @pl.when(seg + d < nseg)
        def _():
            share_copy(d, False).wait_send()


def shards(psi, env_build, env_right, site_left, site_right, charge, rank):
    nseg, nsec = lax.axis_size("seg"), lax.axis_size("sec")
    x = psi[0, 0]
    states, width = x.shape[0], x.shape[2]
    bonds = env_build.shape[2]
    left = site_left.transpose(0, 2, 3, 1)
    right = site_right.transpose(0, 2, 3, 1)
    hbm = pl.BlockSpec(memory_space=pltpu.HBM)
    vmem = pl.BlockSpec(memory_space=pltpu.VMEM)
    dma = pltpu.SemaphoreType.DMA
    nz = nsec // 2
    rows = width // CHUNKS
    slot = pltpu.VMEM((nsec, rows, bonds * width), BF16)
    state, energy, weight = pl.pallas_call(
        functools.partial(kernel, nseg, nsec),
        out_shape=(
            jax.ShapeDtypeStruct(x.shape, BF16),
            jax.ShapeDtypeStruct((1, 1), F32),
            jax.ShapeDtypeStruct((1, 1), F32),
        ),
        in_specs=[hbm] * 7,
        out_specs=(vmem, vmem, vmem),
        scratch_shapes=[
            slot, slot, slot, slot,
            pltpu.VMEM((CHUNKS, rows, bonds * width), BF16),
            pltpu.VMEM(x.shape, BF16),
            pltpu.VMEM((bonds, width, width), BF16),
            pltpu.VMEM((bonds, width, width), BF16),
            pltpu.VMEM(left.shape, BF16),
            pltpu.VMEM(right.shape, BF16),
            pltpu.SMEM(charge.shape, jnp.int32),
            pltpu.SMEM(rank.shape, jnp.int32),
            pltpu.VMEM((rows, bonds * states, width), BF16),
            pltpu.VMEM((states, bonds * width, width), BF16),
            pltpu.VMEM((states, bonds * width, width), BF16),
            pltpu.VMEM((bonds * states, bonds * states), BF16),
            pltpu.VMEM((bonds * states, 128), F32),
            pltpu.VMEM((states * rows, width), F32),
            pltpu.VMEM((states * rows, width), BF16),
            pltpu.VMEM((states, width, width), BF16),
            pltpu.VMEM((states, width, width), F32),
            pltpu.VMEM((ITERS, 3, 8, width), F32),
            pltpu.VMEM((ITERS, nsec, 3, 8, width), F32),
            pltpu.VMEM((8, width), F32),
            pltpu.VMEM((nseg, 8, width), F32),
            pltpu.VMEM((8, width), F32),
            dma((7,)),
            dma((CHUNKS,)),
            dma((CHUNKS, nz)),
            dma((CHUNKS, nz)),
            dma((CHUNKS, nz)),
            dma((CHUNKS, nsec)),
            dma((ITERS, nsec)),
            dma((ITERS, nsec)),
            dma((nseg,)),
            dma((nseg,)),
        ],
        compiler_params=pltpu.CompilerParams(
            collective_id=0, has_side_effects=True, vmem_limit_bytes=64 * 2**20
        ),
    )(x, env_build[0, 0], env_right[0, 0], left, right, charge, rank)
    return (state[None, None], energy.reshape(1), weight.reshape(1, 1))


def solution(mesh):
    return jax.shard_map(
        shards,
        mesh=mesh,
        in_specs=(
            P("seg", "sec", None, None, None),
            P("seg", "sec", None, None, None),
            P("seg", "sec", None, None, None),
            P(),
            P(),
            P(),
            P("sec"),
        ),
        out_specs=(P("seg", "sec", None, None, None), P("seg"), P("seg", "sec")),
        check_vma=False,
    )
```

```python
import functools

import jax
import jax.numpy as jnp
from jax import lax
from jax.experimental import pallas as pl
from jax.experimental.pallas import tpu as pltpu
from jax.sharding import PartitionSpec as P

ITERS = 2
CHUNKS = 4
MESH = pl.DeviceIdType.MESH
F32 = jnp.float32
BF16 = jnp.bfloat16


def dot(a, b):
    return jnp.dot(a, b, preferred_element_type=F32)


def iota(shape, dim):
    return lax.broadcasted_iota(jnp.int32, shape, dim)


def onehot(cond):
    return jnp.where(cond, 1.0, 0.0).astype(BF16)


def fold(values):
    return jnp.sum(values.reshape(-1, 8, values.shape[-1]), axis=0)


def whole_sum(tile):
    return jnp.sum(tile, axis=(0, 1), keepdims=True)


def order_rows(env_ref, lo, rows):
    width = env_ref.shape[2]
    lane = iota((rows, width), 1)
    blocks = []
    for first, per in ((0, 8), (8, 4)):
        parts = [env_ref[first + bond, lo : lo + rows, :].astype(F32) for bond in range(per)]
        for j in range(per):
            block = parts[0] if j == 0 else pltpu.roll(parts[0], width - j, 1)
            for bond in range(1, per):
                turned = parts[bond] if bond == j else pltpu.roll(parts[bond], (bond - j) % width, 1)
                block = jnp.where((lane & (per - 1)) == bond, turned, block)
            blocks.append(block.astype(BF16))
    return blocks


def stage_sites(site_ref, stage):
    stage[...] = jnp.zeros_like(stage)
    local = site_ref.shape[1]
    bonds = site_ref.shape[3]

    def one(bond, carry):
        for new in range(local):
            stage[pl.ds(bond * local * local + new * local, local), 0:bonds] = site_ref[bond, new].astype(F32)
        return carry

    lax.fori_loop(0, site_ref.shape[0], one, 0)


def build_mpo(left_ref, right_ref, stage):
    n = 192
    row = iota((n, 1), 0)
    tail = row >= 128
    q = jnp.where(tail, (row - 128) >> 2, row >> 3)
    bond = jnp.where(tail, 8 + (row & 3), row & 7)
    col = iota((1, n), 1)
    spread = onehot(iota((stage.shape[1], n), 0) == (iota((stage.shape[1], n), 1) >> 4))
    stage_sites(left_ref, stage)
    value = dot(stage[...].astype(BF16), spread)
    value = jnp.where((row & 3) == (col & 3), value, 0.0).astype(BF16)
    value = dot(onehot((bond == (col >> 4)) & ((q >> 2) == ((col >> 2) & 3))), value)
    left = jnp.where((q & 3) == ((col >> 2) & 3), value, 0.0).astype(BF16)
    stage_sites(right_ref, stage)
    value = dot(stage[...].astype(BF16), spread)
    value = jnp.where((row & 3) == (col & 3), value, 0.0).astype(BF16)
    value = dot(onehot(((row >> 4) == (col >> 4)) & (((row >> 2) & 3) == ((col >> 2) & 3))), value)
    right = jnp.where((row & 3) == ((col >> 2) & 3), value, 0.0).astype(BF16)
    return dot(left, right).astype(BF16)


def kernel(
    nseg, nsec,
    psi_hbm, env_hbm, renv_hbm, left_hbm, right_hbm, charge_hbm, rank_hbm,
    state_ref, energy_ref, weight_ref,
    l0, l1, l2, l3, own, psi_ref, env_ref, renv_ref, left_ref, right_ref, charge_ref, rank_ref, x1, x3a, x3b, mpo, stage, flat, xq, acc,
    sum_tx, sum_rx, share_tx, share_rx, run,
    load_sem, shift_sem, up_sem, down_sem, side_sem, recv_sem, sum_send, sum_recv, share_send, share_recv,
):
    seg = lax.axis_index("seg")
    sec = lax.axis_index("sec")
    nz = nsec // 2
    z = sec // 2
    core = sec % 2
    slots = (l0, l1, l2, l3)
    states, width = psi_ref.shape[0], psi_ref.shape[2]
    rows = width // CHUNKS

    pairs = (
        (env_hbm, env_ref), (psi_hbm, psi_ref), (renv_hbm, renv_ref), (left_hbm, left_ref), (right_hbm, right_ref),
        (charge_hbm, charge_ref), (rank_hbm, rank_ref),
    )
    loads = [
        pltpu.make_async_copy(src, dst, load_sem.at[i])
        for i, (src, dst) in enumerate(pairs)
    ]
    for load in loads:
        load.start()

    barrier = pltpu.get_barrier_semaphore()
    for d in range(1, nsec):
        pl.semaphore_signal(barrier, inc=1, device_id=(seg, lax.rem(sec + d, nsec)), device_id_type=MESH)
    for d in range(1, nseg):
        pl.semaphore_signal(barrier, inc=1, device_id=(lax.rem(seg + d, nseg), sec), device_id_type=MESH)

    def copy(src, dst, send, recv, to):
        return pltpu.make_async_remote_copy(
            src_ref=src, dst_ref=dst, send_sem=send, recv_sem=recv, device_id=to, device_id_type=MESH
        )

    def shift(c):
        return copy(own.at[c], slots[c].at[sec], shift_sem.at[c], recv_sem.at[c, sec], (seg + 1, sec))

    def up(c, h):
        s = sec - 2 * h
        return copy(slots[c].at[s], slots[c].at[s], up_sem.at[c, h], recv_sem.at[c, s], (seg, sec + 2))

    def down(c, h):
        s = sec + 2 * h
        return copy(slots[c].at[s], slots[c].at[s], down_sem.at[c, h], recv_sem.at[c, s], (seg, sec - 2))

    def side(c, s):
        return copy(
            slots[c].at[s], slots[c].at[s], side_sem.at[c, s // 2], recv_sem.at[c, s], (seg, sec + 1 - 2 * core)
        )

    def arrived(c, s):
        copy(slots[c].at[s], slots[c].at[s], side_sem.at[c, 0], recv_sem.at[c, s], (seg, sec)).wait_recv()

    def order(c):
        for j, block in enumerate(order_rows(env_ref, c * rows, rows)):
            own[c, :, j * width : (j + 1) * width] = block

        @pl.when(seg == 0)
        def _():
            slots[c][sec] = own[c]

    def shift_out(c):
        @pl.when(seg < nseg - 1)
        def _():
            shift(c).start()

    def hop(c, h):
        if h == 0:
            @pl.when(seg > 0)
            def _():
                arrived(c, sec)

            @pl.when(z < nz - 1)
            def _():
                up(c, 0).start()

            @pl.when(z > 0)
            def _():
                down(c, 0).start()

            side(c, sec).start()
            return

        @pl.when(z >= h)
        def _():
            arrived(c, sec - 2 * h)

            @pl.when(z < nz - 1)
            def _():
                up(c, h).start()

            side(c, sec - 2 * h).start()

        @pl.when(z + h < nz)
        def _():
            arrived(c, sec + 2 * h)

            @pl.when(z > 0)
            def _():
                down(c, h).start()

            side(c, sec + 2 * h).start()

    def settle(c):
        for k in range(nz):
            arrived(c, 2 * k + 1 - core)

    def drain():
        for c in range(CHUNKS):
            @pl.when(seg < nseg - 1)
            def _():
                shift(c).wait_send()

            for h in range(nz):
                @pl.when((z >= h) & (z < nz - 1))
                def _():
                    up(c, h).wait_send()

                @pl.when((z + h < nz) & (z > 0))
                def _():
                    down(c, h).wait_send()

                side(c, 2 * h + core).wait_send()

    def flatten(c):
        for p in range(states):
            flat[pl.ds(p, rows, stride=states), :] = psi_ref[p, c * rows : (c + 1) * rows, :].astype(F32)

    def right_apply(at=0):
        lhs = flat[at * rows * states : (at + 1) * rows * states, :].astype(BF16)
        for w in range(renv_ref.shape[0] // 2):
            rhs = jnp.concatenate([renv_ref[2 * w], renv_ref[2 * w + 1]], axis=1)
            out = dot(lhs, rhs).astype(BF16)
            for half in range(2):
                lo = (2 * w + half) * states
                x1[:, lo : lo + states, :] = out[:, half * width : (half + 1) * width].reshape(rows, states, width)

    def mpo_apply(c, x3):
        group = 16
        low = iota((states // 2, 8, width), 1) < 4

        def one(step, carry):
            operator = mpo[...]
            a = step * group
            at = pl.multiple_of(c * rows + a, group)

            def pair(j):
                out = dot(operator, jnp.concatenate([x1[a + j], x1[a + j + 8]], axis=1))
                parts = [out[:, :width], out[:, width:]]
                heads = [part[:128].reshape(states, 8, width) for part in parts]
                x3[:, pl.ds(pl.multiple_of(j * width + at, 16), 16), :] = jnp.concatenate(heads, axis=1).astype(BF16)
                return [part[128:].reshape(states // 2, 8, width) for part in parts]

            for j in range(4):
                evens, odds = [], []
                for a_tail, b_tail in zip(pair(j), pair(j + 4)):
                    evens.append(jnp.where(low, a_tail, pltpu.roll(b_tail, 4, 1)))
                    odds.append(jnp.where(low, pltpu.roll(a_tail, 4, 1), b_tail))
                even = jnp.concatenate(evens, axis=1).astype(BF16)
                odd = jnp.concatenate(odds, axis=1).astype(BF16)
                both = jnp.stack([even, odd], axis=1).reshape(states, 16, width)
                x3[:, pl.ds(pl.multiple_of((8 + j) * width + at, 16), 16), :] = both
            return carry

        lax.fori_loop(0, rows // group, one, 0)

    def left_of(q):
        return lax.rem(sec - charge_ref[q] + nsec, nsec)

    per = 8
    zero = jnp.zeros((8, width), F32)

    def first(half, squares, keep):
        lo, some_rows = 2 * half * rows, 2 * rows

        def some(step, squares):
            for j in range(per):
                q = step * per + j
                s = left_of(q)
                h = dot(jnp.concatenate([slots[2 * half][s], slots[2 * half + 1][s]], axis=0), x3a[q])
                u = jnp.where(keep, psi_ref[q, lo : lo + some_rows, :].astype(F32) - 0.5 * h, 0.0)
                flat[pl.ds(q, some_rows, stride=states), :] = u
                xq[q, lo : lo + some_rows, :] = u.astype(BF16)
                squares = squares + fold(u * u)
            return squares

        return lax.fori_loop(0, states // per, some, squares)

    def exchange(step):
        for d in range(1, nsec):
            copy(
                sum_tx.at[step], sum_rx.at[step, sec], sum_send.at[step, d], sum_recv.at[step, sec],
                (seg, lax.rem(sec + d, nsec)),
            ).start()

    def collect(step):
        for d in range(1, nsec):
            other = lax.rem(sec + d, nsec)
            copy(
                sum_tx.at[step], sum_rx.at[step, other], sum_send.at[step, d], sum_recv.at[step, other], (seg, other)
            ).wait_recv()
        total = sum_rx[step, 0]
        for other in range(1, nsec):
            total = total + sum_rx[step, other]
        return total

    loads[0].wait()
    order(0)
    pl.semaphore_wait(barrier, nsec + nseg - 2)
    shift_out(0)
    for c in range(1, CHUNKS):
        order(c)
        shift_out(c)
    for load in loads[1:]:
        load.wait()
    mpo[...] = build_mpo(left_ref, right_ref, stage)
    keep = iota((2 * rows, width), 1) < rank_ref[0]
    squares = zero
    finished = 2 * nz - 1
    for t in range(finished + 1):
        for c in range(CHUNKS):
            if (t - c) % 2 == 0 and 0 <= (t - c) // 2 < nz:
                hop(c, (t - c) // 2)
        if t < 2 * CHUNKS:
            if t % 2 == 0:
                flatten(t // 2)
                right_apply()
            else:
                mpo_apply(t // 2, x3a)
    settle(0)
    settle(1)
    squares = first(0, squares, keep)
    for c in range(2):
        right_apply(c)
        mpo_apply(c, x3b)
        hop(c + 2, nz - 1)
        settle(c + 2)
    squares = first(1, squares, keep)
    sums = jnp.stack([squares, zero, zero])
    sum_tx[0] = sums
    sum_rx[0, sec] = sums
    exchange(0)
    for c in range(2):
        right_apply(c)
        mpo_apply(c + 2, x3b)

    count = float(nsec * states * width * width)
    total = collect(0)
    scale = lax.rsqrt(whole_sum(total[0]) / count + 1e-06)

    keep_all = iota((width, width), 1) < rank_ref[0]

    def last(step, carry):
        squares, inner, own_sum = carry
        for j in range(per):
            q = step * per + j
            s = left_of(q)
            h = dot(jnp.concatenate([slot[s] for slot in slots], axis=0), x3b[q]) * scale
            x = xq[q].astype(F32) * scale
            u = jnp.where(keep_all, x - 0.5 * h, 0.0)
            acc[q] = u
            squares = squares + fold(u * u)
            inner = inner + fold(x * h)
            own_sum = own_sum + fold(x * x)
        return squares, inner, own_sum

    sums = lax.fori_loop(0, states // per, last, (zero, zero, zero))
    sum_tx[1] = jnp.stack(sums)
    sum_rx[1, sec] = jnp.stack(sums)
    exchange(1)
    mine = whole_sum(sums[0])
    total = collect(1)
    all_squares = whole_sum(total[0])
    share = jnp.log(float(nsec) * mine / all_squares)
    share_tx[...] = jnp.broadcast_to(share, share_tx.shape)

    def share_copy(d, back):
        there = seg - d if back else seg + d
        slot = share_rx.at[there if back else seg]
        sem = share_recv.at[there if back else seg]
        return copy(share_tx, slot, share_send.at[d], sem, (there, sec))

    for d in range(1, nseg):
        @pl.when(seg + d < nseg)
        def _():
            share_copy(d, False).start()

    scale = lax.rsqrt(all_squares / count + 1e-06)
    energy_ref[...] = whole_sum(total[1]) / whole_sum(total[2])

    def write(q, carry):
        state_ref[q] = (acc[q] * scale).astype(BF16)
        return carry

    lax.fori_loop(0, states, write, 0)
    run[...] = share_tx[...]
    for d in range(1, nseg):
        @pl.when(seg - d >= 0)
        def _():
            share_copy(d, True).wait_recv()
            run[...] += share_rx[seg - d]

    weight_ref[...] = run[0:1, 0:1]
    drain()
    for step in range(ITERS):
        for d in range(1, nsec):
            copy(
                sum_tx.at[step], sum_rx.at[step, sec], sum_send.at[step, d], sum_recv.at[step, sec],
                (seg, lax.rem(sec + d, nsec)),
            ).wait_send()
    for d in range(1, nseg):
        @pl.when(seg + d < nseg)
        def _():
            share_copy(d, False).wait_send()


def shards(psi, env_build, env_right, site_left, site_right, charge, rank):
    nseg, nsec = lax.axis_size("seg"), lax.axis_size("sec")
    x = psi[0, 0]
    states, width = x.shape[0], x.shape[2]
    bonds = env_build.shape[2]
    left = site_left.transpose(0, 2, 3, 1)
    right = site_right.transpose(0, 2, 3, 1)
    hbm = pl.BlockSpec(memory_space=pltpu.HBM)
    vmem = pl.BlockSpec(memory_space=pltpu.VMEM)
    dma = pltpu.SemaphoreType.DMA
    nz = nsec // 2
    rows = width // CHUNKS
    slot = pltpu.VMEM((nsec, rows, bonds * width), BF16)
    state, energy, weight = pl.pallas_call(
        functools.partial(kernel, nseg, nsec),
        out_shape=(
            jax.ShapeDtypeStruct(x.shape, BF16),
            jax.ShapeDtypeStruct((1, 1), F32),
            jax.ShapeDtypeStruct((1, 1), F32),
        ),
        in_specs=[hbm] * 7,
        out_specs=(vmem, vmem, vmem),
        scratch_shapes=[
            slot, slot, slot, slot,
            pltpu.VMEM((CHUNKS, rows, bonds * width), BF16),
            pltpu.VMEM(x.shape, BF16),
            pltpu.VMEM((bonds, width, width), BF16),
            pltpu.VMEM((bonds, width, width), BF16),
            pltpu.VMEM(left.shape, BF16),
            pltpu.VMEM(right.shape, BF16),
            pltpu.SMEM(charge.shape, jnp.int32),
            pltpu.SMEM(rank.shape, jnp.int32),
            pltpu.VMEM((rows, bonds * states, width), BF16),
            pltpu.VMEM((states, bonds * width, width), BF16),
            pltpu.VMEM((states, bonds * width, width), BF16),
            pltpu.VMEM((bonds * states, bonds * states), BF16),
            pltpu.VMEM((bonds * states, 128), F32),
            pltpu.VMEM((2 * states * rows, width), F32),
            pltpu.VMEM((states, width, width), BF16),
            pltpu.VMEM((states, width, width), F32),
            pltpu.VMEM((ITERS, 3, 8, width), F32),
            pltpu.VMEM((ITERS, nsec, 3, 8, width), F32),
            pltpu.VMEM((8, width), F32),
            pltpu.VMEM((nseg, 8, width), F32),
            pltpu.VMEM((8, width), F32),
            dma((7,)),
            dma((CHUNKS,)),
            dma((CHUNKS, nz)),
            dma((CHUNKS, nz)),
            dma((CHUNKS, nz)),
            dma((CHUNKS, nsec)),
            dma((ITERS, nsec)),
            dma((ITERS, nsec)),
            dma((nseg,)),
            dma((nseg,)),
        ],
        compiler_params=pltpu.CompilerParams(
            collective_id=0, has_side_effects=True, vmem_limit_bytes=64 * 2**20
        ),
    )(x, env_build[0, 0], env_right[0, 0], left, right, charge, rank)
    return (state[None, None], energy.reshape(1), weight.reshape(1, 1))


def solution(mesh):
    return jax.shard_map(
        shards,
        mesh=mesh,
        in_specs=(
            P("seg", "sec", None, None, None),
            P("seg", "sec", None, None, None),
            P("seg", "sec", None, None, None),
            P(),
            P(),
            P(),
            P("sec"),
        ),
        out_specs=(P("seg", "sec", None, None, None), P("seg"), P("seg", "sec")),
        check_vma=False,
    )
```

```python
import functools

import jax
import jax.numpy as jnp
from jax import lax
from jax.experimental import pallas as pl
from jax.experimental.pallas import tpu as pltpu
from jax.sharding import PartitionSpec as P

ITERS = 2
CHUNKS = 4
MESH = pl.DeviceIdType.MESH
F32 = jnp.float32
BF16 = jnp.bfloat16


def dot(a, b):
    return jnp.dot(a, b, preferred_element_type=F32)


def iota(shape, dim):
    return lax.broadcasted_iota(jnp.int32, shape, dim)


def onehot(cond):
    return jnp.where(cond, 1.0, 0.0).astype(BF16)


def fold(values):
    return jnp.sum(values.reshape(-1, 8, values.shape[-1]), axis=0)


def whole_sum(tile):
    return jnp.sum(tile, axis=(0, 1), keepdims=True)


def order_rows(env_ref, lo, rows):
    width = env_ref.shape[2]
    lane = iota((rows, width), 1)
    blocks = []
    for first, per in ((0, 8), (8, 4)):
        parts = [env_ref[first + bond, lo : lo + rows, :].astype(F32) for bond in range(per)]
        for j in range(per):
            block = parts[0] if j == 0 else pltpu.roll(parts[0], width - j, 1)
            for bond in range(1, per):
                turned = parts[bond] if bond == j else pltpu.roll(parts[bond], (bond - j) % width, 1)
                block = jnp.where((lane & (per - 1)) == bond, turned, block)
            blocks.append(block.astype(BF16))
    return blocks


def stage_sites(site_ref, stage):
    stage[...] = jnp.zeros_like(stage)
    local = site_ref.shape[1]
    bonds = site_ref.shape[3]

    def one(bond, carry):
        for new in range(local):
            stage[pl.ds(bond * local * local + new * local, local), 0:bonds] = site_ref[bond, new].astype(F32)
        return carry

    lax.fori_loop(0, site_ref.shape[0], one, 0)


def build_mpo(left_ref, right_ref, stage):
    n = 192
    row = iota((n, 1), 0)
    tail = row >= 128
    q = jnp.where(tail, (row - 128) >> 2, row >> 3)
    bond = jnp.where(tail, 8 + (row & 3), row & 7)
    col = iota((1, n), 1)
    spread = onehot(iota((stage.shape[1], n), 0) == (iota((stage.shape[1], n), 1) >> 4))
    stage_sites(left_ref, stage)
    value = dot(stage[...].astype(BF16), spread)
    value = jnp.where((row & 3) == (col & 3), value, 0.0).astype(BF16)
    value = dot(onehot((bond == (col >> 4)) & ((q >> 2) == ((col >> 2) & 3))), value)
    left = jnp.where((q & 3) == ((col >> 2) & 3), value, 0.0).astype(BF16)
    stage_sites(right_ref, stage)
    value = dot(stage[...].astype(BF16), spread)
    value = jnp.where((row & 3) == (col & 3), value, 0.0).astype(BF16)
    value = dot(onehot(((row >> 4) == (col >> 4)) & (((row >> 2) & 3) == ((col >> 2) & 3))), value)
    right = jnp.where((row & 3) == ((col >> 2) & 3), value, 0.0).astype(BF16)
    return dot(left, right).astype(BF16)


def kernel(
    nseg, nsec,
    psi_hbm, env_hbm, renv_hbm, left_hbm, right_hbm, charge_hbm, rank_hbm,
    state_ref, scale_ref, energy_ref, weight_ref,
    l0, l1, l2, l3, own, psi_ref, env_ref, renv_ref, left_ref, right_ref, charge_ref, rank_ref, x1, x3, mpo, stage, flat, xq, acc,
    sum_tx, sum_rx, share_tx, share_rx, run,
    load_sem, out_sem, shift_sem, up_sem, down_sem, side_sem, recv_sem, sum_send, sum_recv, share_send, share_recv,
):
    seg = lax.axis_index("seg")
    sec = lax.axis_index("sec")
    nz = nsec // 2
    z = sec // 2
    core = sec % 2
    slots = (l0, l1, l2, l3)
    states, width = psi_ref.shape[0], psi_ref.shape[2]
    rows = width // CHUNKS

    pairs = (
        (env_hbm, env_ref), (psi_hbm, psi_ref), (renv_hbm, renv_ref), (left_hbm, left_ref), (right_hbm, right_ref),
        (charge_hbm, charge_ref), (rank_hbm, rank_ref),
    )
    loads = [
        pltpu.make_async_copy(src, dst, load_sem.at[i])
        for i, (src, dst) in enumerate(pairs)
    ]
    for load in loads:
        load.start()

    barrier = pltpu.get_barrier_semaphore()
    for d in range(1, nsec):
        pl.semaphore_signal(barrier, inc=1, device_id=(seg, lax.rem(sec + d, nsec)), device_id_type=MESH)
    for d in range(1, nseg):
        pl.semaphore_signal(barrier, inc=1, device_id=(lax.rem(seg + d, nseg), sec), device_id_type=MESH)

    def copy(src, dst, send, recv, to):
        return pltpu.make_async_remote_copy(
            src_ref=src, dst_ref=dst, send_sem=send, recv_sem=recv, device_id=to, device_id_type=MESH
        )

    def shift(c):
        return copy(own.at[c], slots[c].at[sec], shift_sem.at[c], recv_sem.at[c, sec], (seg + 1, sec))

    def up(c, h):
        s = sec - 2 * h
        return copy(slots[c].at[s], slots[c].at[s], up_sem.at[c, h], recv_sem.at[c, s], (seg, sec + 2))

    def down(c, h):
        s = sec + 2 * h
        return copy(slots[c].at[s], slots[c].at[s], down_sem.at[c, h], recv_sem.at[c, s], (seg, sec - 2))

    def side(c, s):
        return copy(
            slots[c].at[s], slots[c].at[s], side_sem.at[c, s // 2], recv_sem.at[c, s], (seg, sec + 1 - 2 * core)
        )

    def arrived(c, s):
        copy(slots[c].at[s], slots[c].at[s], side_sem.at[c, 0], recv_sem.at[c, s], (seg, sec)).wait_recv()

    def order(c):
        for j, block in enumerate(order_rows(env_ref, c * rows, rows)):
            own[c, :, j * width : (j + 1) * width] = block

        @pl.when(seg == 0)
        def _():
            slots[c][sec] = own[c]

    def shift_out(c):
        @pl.when(seg < nseg - 1)
        def _():
            shift(c).start()

    def hop(c, h):
        if h == 0:
            @pl.when(seg > 0)
            def _():
                arrived(c, sec)

            @pl.when(z < nz - 1)
            def _():
                up(c, 0).start()

            @pl.when(z > 0)
            def _():
                down(c, 0).start()

            side(c, sec).start()
            return

        @pl.when(z >= h)
        def _():
            arrived(c, sec - 2 * h)

            @pl.when(z < nz - 1)
            def _():
                up(c, h).start()

            side(c, sec - 2 * h).start()

        @pl.when(z + h < nz)
        def _():
            arrived(c, sec + 2 * h)

            @pl.when(z > 0)
            def _():
                down(c, h).start()

            side(c, sec + 2 * h).start()

    def settle(c):
        for k in range(nz):
            arrived(c, 2 * k + 1 - core)

    def drain():
        for c in range(CHUNKS):
            @pl.when(seg < nseg - 1)
            def _():
                shift(c).wait_send()

            for h in range(nz):
                @pl.when((z >= h) & (z < nz - 1))
                def _():
                    up(c, h).wait_send()

                @pl.when((z + h < nz) & (z > 0))
                def _():
                    down(c, h).wait_send()

                side(c, 2 * h + core).wait_send()

    def flatten(c):
        lo = pl.multiple_of(c * rows, rows)
        at = lax.rem(c, 2) * rows * states
        for p in range(states):
            flat[pl.ds(at + p, rows, stride=states), :] = psi_ref[p, pl.ds(lo, rows), :].astype(F32)

    def right_apply(c):
        at = pl.multiple_of(lax.rem(c, 2) * rows * states, rows * states)
        lhs = flat[pl.ds(at, rows * states), :].astype(BF16)
        for w in range(renv_ref.shape[0] // 2):
            rhs = jnp.concatenate([renv_ref[2 * w], renv_ref[2 * w + 1]], axis=1)
            out = dot(lhs, rhs).astype(BF16)
            for half in range(2):
                lo = (2 * w + half) * states
                x1[:, lo : lo + states, :] = out[:, half * width : (half + 1) * width].reshape(rows, states, width)

    def mpo_apply(c, turn):
        group = 16
        low = iota((states // 2, 8, width), 1) < 4

        def one(step, carry):
            operator = mpo[...]
            a = step * group
            at = pl.multiple_of(c * rows + a, group)

            def pair(j):
                out = dot(operator, jnp.concatenate([x1[a + j], x1[a + j + 8]], axis=1))
                parts = [out[:, :width], out[:, width:]]
                heads = [part[:128].reshape(states, 8, width) for part in parts]
                x3[turn, :, pl.ds(pl.multiple_of(j * width + at, 16), 16), :] = jnp.concatenate(heads, axis=1).astype(BF16)
                return [part[128:].reshape(states // 2, 8, width) for part in parts]

            for j in range(4):
                evens, odds = [], []
                for a_tail, b_tail in zip(pair(j), pair(j + 4)):
                    evens.append(jnp.where(low, a_tail, pltpu.roll(b_tail, 4, 1)))
                    odds.append(jnp.where(low, pltpu.roll(a_tail, 4, 1), b_tail))
                even = jnp.concatenate(evens, axis=1).astype(BF16)
                odd = jnp.concatenate(odds, axis=1).astype(BF16)
                both = jnp.stack([even, odd], axis=1).reshape(states, 16, width)
                x3[turn, :, pl.ds(pl.multiple_of((8 + j) * width + at, 16), 16), :] = both
            return carry

        lax.fori_loop(0, rows // group, one, 0)

    def left_of(q):
        return lax.rem(sec - charge_ref[q] + nsec, nsec)

    per = 8
    zero = jnp.zeros((8, width), F32)

    def first(half, keep):
        lo, some_rows = 2 * half * rows, 2 * rows

        def some(step, squares):
            for j in range(per):
                q = step * per + j
                s = left_of(q)
                h = dot(jnp.concatenate([slots[2 * half][s], slots[2 * half + 1][s]], axis=0), x3[0, q])
                u = jnp.where(keep, psi_ref[q, lo : lo + some_rows, :].astype(F32) - 0.5 * h, 0.0)
                flat[pl.ds(q, some_rows, stride=states), :] = u
                xq[q, lo : lo + some_rows, :] = u.astype(BF16)
                squares = squares + fold(u * u)
            return squares

        sum_tx[0, 0] += lax.fori_loop(0, states // per, some, zero)

    def exchange(step):
        for d in range(1, nsec):
            copy(
                sum_tx.at[step], sum_rx.at[step, sec], sum_send.at[step, d], sum_recv.at[step, sec],
                (seg, lax.rem(sec + d, nsec)),
            ).start()

    def collect(step):
        for d in range(1, nsec):
            other = lax.rem(sec + d, nsec)
            copy(
                sum_tx.at[step], sum_rx.at[step, other], sum_send.at[step, d], sum_recv.at[step, other], (seg, other)
            ).wait_recv()
        total = sum_rx[step, 0]
        for other in range(1, nsec):
            total = total + sum_rx[step, other]
        return total

    loads[0].wait()
    order(0)
    pl.semaphore_wait(barrier, nsec + nseg - 2)
    shift_out(0)
    for c in range(1, CHUNKS):
        order(c)
        shift_out(c)
    for load in loads[1:]:
        load.wait()
    mpo[...] = build_mpo(left_ref, right_ref, stage)
    keep = iota((2 * rows, width), 1) < rank_ref[0]
    finished = 2 * nz - 1

    def group(t):
        for c in range(CHUNKS):
            if (t - c) % 2 == 0 and 0 <= (t - c) // 2 < nz:
                hop(c, (t - c) // 2)

    def piece(i, carry):
        c = lax.rem(i, CHUNKS)
        for k in range(CHUNKS):
            @pl.when(i == k)
            def _():
                group(2 * k)

        @pl.when(i < CHUNKS)
        def _():
            flatten(c)

        @pl.when(i == CHUNKS)
        def _():
            for t in range(2 * CHUNKS, finished + 1):
                group(t)
            settle(0)
            settle(1)
            first(0, keep)

        @pl.when(i == CHUNKS + 1)
        def _():
            hop(2, nz - 1)

        @pl.when(i == CHUNKS + 2)
        def _():
            hop(3, nz - 1)
            settle(2)
            settle(3)
            first(1, keep)
            sum_rx[0, sec] = sum_tx[0]
            exchange(0)

        right_apply(c)
        for k in range(CHUNKS):
            @pl.when(i == k)
            def _():
                group(2 * k + 1)

        mpo_apply(c, i // CHUNKS)
        return carry

    sum_tx[0] = jnp.zeros_like(sum_tx[0])
    lax.fori_loop(0, 2 * CHUNKS, piece, 0)

    count = float(nsec * states * width * width)
    total = collect(0)
    scale = lax.rsqrt(whole_sum(total[0]) / count + 1e-06)

    def result(step):
        some = pl.ds(step * per, per)
        return pltpu.make_async_copy(acc.at[some], state_ref.at[some], out_sem.at[step])

    keep_all = iota((width, width), 1) < rank_ref[0]

    def last(step, carry):
        squares, inner, own_sum = carry
        for j in range(per):
            q = step * per + j
            s = left_of(q)
            h = dot(jnp.concatenate([slot[s] for slot in slots], axis=0), x3[1, q]) * scale
            x = xq[q].astype(F32) * scale
            u = jnp.where(keep_all, x - 0.5 * h, 0.0)
            acc[q] = u
            squares = squares + fold(u * u)
            inner = inner + fold(x * h)
            own_sum = own_sum + fold(x * x)
        result(step).start()
        return squares, inner, own_sum

    sums = lax.fori_loop(0, states // per, last, (zero, zero, zero))
    sum_tx[1] = jnp.stack(sums)
    sum_rx[1, sec] = jnp.stack(sums)
    exchange(1)
    mine = whole_sum(sums[0])
    total = collect(1)
    all_squares = whole_sum(total[0])
    share = jnp.log(float(nsec) * mine / all_squares)
    share_tx[...] = jnp.broadcast_to(share, share_tx.shape)

    def share_copy(d, back):
        there = seg - d if back else seg + d
        slot = share_rx.at[there if back else seg]
        sem = share_recv.at[there if back else seg]
        return copy(share_tx, slot, share_send.at[d], sem, (there, sec))

    for d in range(1, nseg):
        @pl.when(seg + d < nseg)
        def _():
            share_copy(d, False).start()

    scale_ref[...] = lax.rsqrt(all_squares / count + 1e-06)
    energy_ref[...] = whole_sum(total[1]) / whole_sum(total[2])
    drain()
    for step in range(ITERS):
        for d in range(1, nsec):
            copy(
                sum_tx.at[step], sum_rx.at[step, sec], sum_send.at[step, d], sum_recv.at[step, sec],
                (seg, lax.rem(sec + d, nsec)),
            ).wait_send()
    for d in range(1, nseg):
        @pl.when(seg + d < nseg)
        def _():
            share_copy(d, False).wait_send()

    run[...] = share_tx[...]
    for d in range(1, nseg):
        @pl.when(seg - d >= 0)
        def _():
            share_copy(d, True).wait_recv()
            run[...] += share_rx[seg - d]

    weight_ref[...] = run[0:1, 0:1]
    for step in range(states // per):
        result(step).wait()


def shards(psi, env_build, env_right, site_left, site_right, charge, rank):
    nseg, nsec = lax.axis_size("seg"), lax.axis_size("sec")
    x = psi[0, 0]
    states, width = x.shape[0], x.shape[2]
    bonds = env_build.shape[2]
    left = site_left.transpose(0, 2, 3, 1)
    right = site_right.transpose(0, 2, 3, 1)
    hbm = pl.BlockSpec(memory_space=pltpu.HBM)
    vmem = pl.BlockSpec(memory_space=pltpu.VMEM)
    dma = pltpu.SemaphoreType.DMA
    nz = nsec // 2
    rows = width // CHUNKS
    slot = pltpu.VMEM((nsec, rows, bonds * width), BF16)
    state, scale, energy, weight = pl.pallas_call(
        functools.partial(kernel, nseg, nsec),
        out_shape=(
            jax.ShapeDtypeStruct(x.shape, F32),
            jax.ShapeDtypeStruct((1, 1), F32),
            jax.ShapeDtypeStruct((1, 1), F32),
            jax.ShapeDtypeStruct((1, 1), F32),
        ),
        in_specs=[hbm] * 7,
        out_specs=(hbm, vmem, vmem, vmem),
        scratch_shapes=[
            slot, slot, slot, slot,
            pltpu.VMEM((CHUNKS, rows, bonds * width), BF16),
            pltpu.VMEM(x.shape, BF16),
            pltpu.VMEM((bonds, width, width), BF16),
            pltpu.VMEM((bonds, width, width), BF16),
            pltpu.VMEM(left.shape, BF16),
            pltpu.VMEM(right.shape, BF16),
            pltpu.SMEM(charge.shape, jnp.int32),
            pltpu.SMEM(rank.shape, jnp.int32),
            pltpu.VMEM((rows, bonds * states, width), BF16),
            pltpu.VMEM((ITERS, states, bonds * width, width), BF16),
            pltpu.VMEM((bonds * states, bonds * states), BF16),
            pltpu.VMEM((bonds * states, 128), F32),
            pltpu.VMEM((2 * states * rows, width), F32),
            pltpu.VMEM((states, width, width), BF16),
            pltpu.VMEM((states, width, width), F32),
            pltpu.VMEM((ITERS, 3, 8, width), F32),
            pltpu.VMEM((ITERS, nsec, 3, 8, width), F32),
            pltpu.VMEM((8, width), F32),
            pltpu.VMEM((nseg, 8, width), F32),
            pltpu.VMEM((8, width), F32),
            dma((7,)),
            dma((2,)),
            dma((CHUNKS,)),
            dma((CHUNKS, nz)),
            dma((CHUNKS, nz)),
            dma((CHUNKS, nz)),
            dma((CHUNKS, nsec)),
            dma((ITERS, nsec)),
            dma((ITERS, nsec)),
            dma((nseg,)),
            dma((nseg,)),
        ],
        compiler_params=pltpu.CompilerParams(
            collective_id=0, has_side_effects=True, vmem_limit_bytes=64 * 2**20
        ),
    )(x, env_build[0, 0], env_right[0, 0], left, right, charge, rank)
    state = (state * scale).astype(BF16)
    return (state[None, None], energy.reshape(1), weight.reshape(1, 1))


def solution(mesh):
    return jax.shard_map(
        shards,
        mesh=mesh,
        in_specs=(
            P("seg", "sec", None, None, None),
            P("seg", "sec", None, None, None),
            P("seg", "sec", None, None, None),
            P(),
            P(),
            P(),
            P("sec"),
        ),
        out_specs=(P("seg", "sec", None, None, None), P("seg"), P("seg", "sec")),
        check_vma=False,
    )
```

```python
import functools

import jax
import jax.numpy as jnp
from jax import lax
from jax.experimental import pallas as pl
from jax.experimental.pallas import tpu as pltpu
from jax.sharding import PartitionSpec as P

ITERS = 2
CHUNKS = 4
MESH = pl.DeviceIdType.MESH
F32 = jnp.float32
BF16 = jnp.bfloat16


def dot(a, b):
    return jnp.dot(a, b, preferred_element_type=F32)


def iota(shape, dim):
    return lax.broadcasted_iota(jnp.int32, shape, dim)


def onehot(cond):
    return jnp.where(cond, 1.0, 0.0).astype(BF16)


def fold(values):
    return jnp.sum(values.reshape(-1, 8, values.shape[-1]), axis=0)


def whole_sum(tile):
    return jnp.sum(tile, axis=(0, 1), keepdims=True)


def order_rows(env_ref, lo, rows):
    width = env_ref.shape[2]
    lane = iota((rows, width), 1)
    blocks = []
    for first, per in ((0, 8), (8, 4)):
        parts = [env_ref[first + bond, lo : lo + rows, :].astype(F32) for bond in range(per)]
        for j in range(per):
            block = parts[0] if j == 0 else pltpu.roll(parts[0], width - j, 1)
            for bond in range(1, per):
                turned = parts[bond] if bond == j else pltpu.roll(parts[bond], (bond - j) % width, 1)
                block = jnp.where((lane & (per - 1)) == bond, turned, block)
            blocks.append(block.astype(BF16))
    return blocks


def stage_sites(site_ref, stage):
    stage[...] = jnp.zeros_like(stage)
    local = site_ref.shape[1]
    bonds = site_ref.shape[3]

    def one(bond, carry):
        for new in range(local):
            stage[pl.ds(bond * local * local + new * local, local), 0:bonds] = site_ref[bond, new].astype(F32)
        return carry

    lax.fori_loop(0, site_ref.shape[0], one, 0)


def build_mpo(left_ref, right_ref, stage):
    n = 192
    row = iota((n, 1), 0)
    tail = row >= 128
    q = jnp.where(tail, (row - 128) >> 2, row >> 3)
    bond = jnp.where(tail, 8 + (row & 3), row & 7)
    col = iota((1, n), 1)
    spread = onehot(iota((stage.shape[1], n), 0) == (iota((stage.shape[1], n), 1) >> 4))
    stage_sites(left_ref, stage)
    value = dot(stage[...].astype(BF16), spread)
    value = jnp.where((row & 3) == (col & 3), value, 0.0).astype(BF16)
    value = dot(onehot((bond == (col >> 4)) & ((q >> 2) == ((col >> 2) & 3))), value)
    left = jnp.where((q & 3) == ((col >> 2) & 3), value, 0.0).astype(BF16)
    stage_sites(right_ref, stage)
    value = dot(stage[...].astype(BF16), spread)
    value = jnp.where((row & 3) == (col & 3), value, 0.0).astype(BF16)
    value = dot(onehot(((row >> 4) == (col >> 4)) & (((row >> 2) & 3) == ((col >> 2) & 3))), value)
    right = jnp.where((row & 3) == ((col >> 2) & 3), value, 0.0).astype(BF16)
    return dot(left, right).astype(BF16)


def kernel(
    nseg, nsec,
    psi_hbm, env_hbm, renv_hbm, left_hbm, right_hbm, charge_hbm, rank_hbm,
    state_ref, scale_ref, energy_ref, weight_ref,
    l0, l1, l2, l3, own, psi_ref, env_ref, renv_ref, left_ref, right_ref, charge_ref, rank_ref, x1, x3, mpo, stage, flat, xq, acc,
    sum_tx, sum_rx, share_tx, share_rx, run,
    load_sem, out_sem, shift_sem, up_sem, down_sem, side_sem, recv_sem, sum_send, sum_recv, share_send, share_recv,
):
    seg = lax.axis_index("seg")
    sec = lax.axis_index("sec")
    nz = nsec // 2
    z = sec // 2
    core = sec % 2
    slots = (l0, l1, l2, l3)
    states, width = psi_ref.shape[0], psi_ref.shape[2]
    rows = width // CHUNKS

    pairs = (
        (env_hbm, env_ref), (psi_hbm, psi_ref), (renv_hbm, renv_ref), (left_hbm, left_ref), (right_hbm, right_ref),
        (charge_hbm, charge_ref), (rank_hbm, rank_ref),
    )
    loads = [
        pltpu.make_async_copy(src, dst, load_sem.at[i])
        for i, (src, dst) in enumerate(pairs)
    ]
    for load in loads:
        load.start()

    barrier = pltpu.get_barrier_semaphore()
    for d in range(1, nsec):
        pl.semaphore_signal(barrier, inc=1, device_id=(seg, lax.rem(sec + d, nsec)), device_id_type=MESH)
    for d in range(1, nseg):
        pl.semaphore_signal(barrier, inc=1, device_id=(lax.rem(seg + d, nseg), sec), device_id_type=MESH)

    def copy(src, dst, send, recv, to):
        return pltpu.make_async_remote_copy(
            src_ref=src, dst_ref=dst, send_sem=send, recv_sem=recv, device_id=to, device_id_type=MESH
        )

    def shift(c):
        return copy(own.at[c], slots[c].at[sec], shift_sem.at[c], recv_sem.at[c, sec], (seg + 1, sec))

    def up(c, h):
        s = sec - 2 * h
        return copy(slots[c].at[s], slots[c].at[s], up_sem.at[c, h], recv_sem.at[c, s], (seg, sec + 2))

    def down(c, h):
        s = sec + 2 * h
        return copy(slots[c].at[s], slots[c].at[s], down_sem.at[c, h], recv_sem.at[c, s], (seg, sec - 2))

    def side(c, s):
        return copy(
            slots[c].at[s], slots[c].at[s], side_sem.at[c, s // 2], recv_sem.at[c, s], (seg, sec + 1 - 2 * core)
        )

    def arrived(c, s):
        copy(slots[c].at[s], slots[c].at[s], side_sem.at[c, 0], recv_sem.at[c, s], (seg, sec)).wait_recv()

    def order(c):
        for j, block in enumerate(order_rows(env_ref, c * rows, rows)):
            own[c, :, j * width : (j + 1) * width] = block

        @pl.when(seg == 0)
        def _():
            slots[c][sec] = own[c]

    def shift_out(c):
        @pl.when(seg < nseg - 1)
        def _():
            shift(c).start()

    def hop(c, h):
        if h == 0:
            @pl.when(seg > 0)
            def _():
                arrived(c, sec)

            @pl.when(z < nz - 1)
            def _():
                up(c, 0).start()

            @pl.when(z > 0)
            def _():
                down(c, 0).start()

            side(c, sec).start()
            return

        @pl.when(z >= h)
        def _():
            arrived(c, sec - 2 * h)

            @pl.when(z < nz - 1)
            def _():
                up(c, h).start()

            side(c, sec - 2 * h).start()

        @pl.when(z + h < nz)
        def _():
            arrived(c, sec + 2 * h)

            @pl.when(z > 0)
            def _():
                down(c, h).start()

            side(c, sec + 2 * h).start()

    def settle(c):
        for k in range(nz):
            arrived(c, 2 * k + 1 - core)

    def drain():
        for c in range(CHUNKS):
            @pl.when(seg < nseg - 1)
            def _():
                shift(c).wait_send()

            for h in range(nz):
                @pl.when((z >= h) & (z < nz - 1))
                def _():
                    up(c, h).wait_send()

                @pl.when((z + h < nz) & (z > 0))
                def _():
                    down(c, h).wait_send()

                side(c, 2 * h + core).wait_send()

    def flatten(c):
        lo = pl.multiple_of(c * rows, rows)
        at = lax.rem(c, 2) * rows * states
        for p in range(states):
            flat[pl.ds(at + p, rows, stride=states), :] = psi_ref[p, pl.ds(lo, rows), :].astype(F32)

    def right_apply(c):
        at = pl.multiple_of(lax.rem(c, 2) * rows * states, rows * states)
        lhs = flat[pl.ds(at, rows * states), :].astype(BF16)
        for w in range(renv_ref.shape[0] // 2):
            rhs = jnp.concatenate([renv_ref[2 * w], renv_ref[2 * w + 1]], axis=1)
            out = dot(lhs, rhs).astype(BF16)
            for half in range(2):
                lo = (2 * w + half) * states
                x1[:, lo : lo + states, :] = out[:, half * width : (half + 1) * width].reshape(rows, states, width)

    def mpo_apply(c, turn):
        group = 16
        low = iota((states // 2, 8, width), 1) < 4

        def one(step, carry):
            operator = mpo[...]
            a = step * group
            at = pl.multiple_of(c * rows + a, group)

            def pair(j):
                out = dot(operator, jnp.concatenate([x1[a + j], x1[a + j + 8]], axis=1))
                parts = [out[:, :width], out[:, width:]]
                heads = [part[:128].reshape(states, 8, width) for part in parts]
                x3[turn, :, pl.ds(pl.multiple_of(j * width + at, 16), 16), :] = jnp.concatenate(heads, axis=1).astype(BF16)
                return [part[128:].reshape(states // 2, 8, width) for part in parts]

            for j in range(4):
                evens, odds = [], []
                for a_tail, b_tail in zip(pair(j), pair(j + 4)):
                    evens.append(jnp.where(low, a_tail, pltpu.roll(b_tail, 4, 1)))
                    odds.append(jnp.where(low, pltpu.roll(a_tail, 4, 1), b_tail))
                even = jnp.concatenate(evens, axis=1).astype(BF16)
                odd = jnp.concatenate(odds, axis=1).astype(BF16)
                both = jnp.stack([even, odd], axis=1).reshape(states, 16, width)
                x3[turn, :, pl.ds(pl.multiple_of((8 + j) * width + at, 16), 16), :] = both
            return carry

        lax.fori_loop(0, rows // group, one, 0)

    def left_of(q):
        return lax.rem(sec - charge_ref[q] + nsec, nsec)

    per = 8
    zero = jnp.zeros((8, width), F32)

    def first(half, part, keep):
        lo, some_rows = 2 * half * rows, 2 * rows

        def some(step, squares):
            for j in range(per):
                q = step * per + j
                s = left_of(q)
                h = dot(jnp.concatenate([slots[2 * half][s], slots[2 * half + 1][s]], axis=0), x3[0, q])
                u = jnp.where(keep, psi_ref[q, lo : lo + some_rows, :].astype(F32) - 0.5 * h, 0.0)
                flat[pl.ds(q, some_rows, stride=states), :] = u
                xq[q, lo : lo + some_rows, :] = u.astype(BF16)
                squares = squares + fold(u * u)
            return squares

        sum_tx[0, 0] += some(part, zero)

    def exchange(step):
        for d in range(1, nsec):
            copy(
                sum_tx.at[step], sum_rx.at[step, sec], sum_send.at[step, d], sum_recv.at[step, sec],
                (seg, lax.rem(sec + d, nsec)),
            ).start()

    def collect(step):
        for d in range(1, nsec):
            other = lax.rem(sec + d, nsec)
            copy(
                sum_tx.at[step], sum_rx.at[step, other], sum_send.at[step, d], sum_recv.at[step, other], (seg, other)
            ).wait_recv()
        total = sum_rx[step, 0]
        for other in range(1, nsec):
            total = total + sum_rx[step, other]
        return total

    loads[0].wait()
    order(0)
    pl.semaphore_wait(barrier, nsec + nseg - 2)
    shift_out(0)
    for c in range(1, CHUNKS):
        order(c)
        shift_out(c)
    for load in loads[1:]:
        load.wait()
    mpo[...] = build_mpo(left_ref, right_ref, stage)
    keep = iota((2 * rows, width), 1) < rank_ref[0]
    end = nz - 1

    def both(pair, h_lo, h_hi):
        return [(c, h) for h in range(h_lo, h_hi) for c in pair]

    before_right = {
        0: [(0, 0)],
        1: [(1, 1)],
        2: [(0, 2)],
        3: [(2, 0)],
        4: [(3, 0), (1, end)],
        5: [(2, 2)],
        6: both((2, 3), 3, end) + [(2, end), (3, end)],
    }
    before_mpo = {
        0: [(1, 0), (0, 1)],
        2: both((0, 1), 2, end)[1:],
        3: [(0, end)],
        4: [(3, 1)],
        5: [(3, 2)],
    }

    def hops(i, table):
        for k, some in table.items():
            @pl.when(i == k)
            def _():
                for c, h in some:
                    hop(c, h)

    def piece(i, carry):
        c = lax.rem(i, CHUNKS)
        hops(i, before_right)

        @pl.when(i < CHUNKS)
        def _():
            flatten(c)

        @pl.when(i == CHUNKS)
        def _():
            settle(0)
            settle(1)
            first(0, 0, keep)
            hop(2, 1)
            first(0, 1, keep)

        @pl.when(i == CHUNKS + 2)
        def _():
            settle(2)
            settle(3)
            first(1, 0, keep)
            first(1, 1, keep)
            sum_rx[0, sec] = sum_tx[0]
            exchange(0)

        right_apply(c)
        hops(i, before_mpo)
        mpo_apply(c, i // CHUNKS)
        return carry

    sum_tx[0] = jnp.zeros_like(sum_tx[0])
    lax.fori_loop(0, 2 * CHUNKS, piece, 0)

    count = float(nsec * states * width * width)
    total = collect(0)
    scale = lax.rsqrt(whole_sum(total[0]) / count + 1e-06)

    def result(step):
        some = pl.ds(step * per, per)
        return pltpu.make_async_copy(acc.at[some], state_ref.at[some], out_sem.at[step])

    keep_all = iota((width, width), 1) < rank_ref[0]

    def last(step, carry):
        squares, inner, own_sum = carry
        for j in range(per):
            q = step * per + j
            s = left_of(q)
            h = dot(jnp.concatenate([slot[s] for slot in slots], axis=0), x3[1, q]) * scale
            x = xq[q].astype(F32) * scale
            u = jnp.where(keep_all, x - 0.5 * h, 0.0)
            acc[q] = u.astype(BF16)
            squares = squares + fold(u * u)
            inner = inner + fold(x * h)
            own_sum = own_sum + fold(x * x)
        result(step).start()
        return squares, inner, own_sum

    sums = lax.fori_loop(0, states // per, last, (zero, zero, zero))
    sum_tx[1] = jnp.stack(sums)
    sum_rx[1, sec] = jnp.stack(sums)
    exchange(1)
    mine = whole_sum(sums[0])
    total = collect(1)
    all_squares = whole_sum(total[0])
    share = jnp.log(float(nsec) * mine / all_squares)
    share_tx[...] = jnp.broadcast_to(share, share_tx.shape)

    def share_copy(d, back):
        there = seg - d if back else seg + d
        slot = share_rx.at[there if back else seg]
        sem = share_recv.at[there if back else seg]
        return copy(share_tx, slot, share_send.at[d], sem, (there, sec))

    for d in range(1, nseg):
        @pl.when(seg + d < nseg)
        def _():
            share_copy(d, False).start()

    scale_ref[...] = lax.rsqrt(all_squares / count + 1e-06)
    energy_ref[...] = whole_sum(total[1]) / whole_sum(total[2])
    drain()
    for step in range(ITERS):
        for d in range(1, nsec):
            copy(
                sum_tx.at[step], sum_rx.at[step, sec], sum_send.at[step, d], sum_recv.at[step, sec],
                (seg, lax.rem(sec + d, nsec)),
            ).wait_send()
    for d in range(1, nseg):
        @pl.when(seg + d < nseg)
        def _():
            share_copy(d, False).wait_send()

    run[...] = share_tx[...]
    for d in range(1, nseg):
        @pl.when(seg - d >= 0)
        def _():
            share_copy(d, True).wait_recv()
            run[...] += share_rx[seg - d]

    weight_ref[...] = run[0:1, 0:1]
    for step in range(states // per):
        result(step).wait()


def shards(psi, env_build, env_right, site_left, site_right, charge, rank):
    nseg, nsec = lax.axis_size("seg"), lax.axis_size("sec")
    x = psi[0, 0]
    states, width = x.shape[0], x.shape[2]
    bonds = env_build.shape[2]
    left = site_left.transpose(0, 2, 3, 1)
    right = site_right.transpose(0, 2, 3, 1)
    hbm = pl.BlockSpec(memory_space=pltpu.HBM)
    vmem = pl.BlockSpec(memory_space=pltpu.VMEM)
    dma = pltpu.SemaphoreType.DMA
    nz = nsec // 2
    rows = width // CHUNKS
    slot = pltpu.VMEM((nsec, rows, bonds * width), BF16)
    state, scale, energy, weight = pl.pallas_call(
        functools.partial(kernel, nseg, nsec),
        out_shape=(
            jax.ShapeDtypeStruct(x.shape, BF16),
            jax.ShapeDtypeStruct((1, 1), F32),
            jax.ShapeDtypeStruct((1, 1), F32),
            jax.ShapeDtypeStruct((1, 1), F32),
        ),
        in_specs=[hbm] * 7,
        out_specs=(hbm, vmem, vmem, vmem),
        scratch_shapes=[
            slot, slot, slot, slot,
            pltpu.VMEM((CHUNKS, rows, bonds * width), BF16),
            pltpu.VMEM(x.shape, BF16),
            pltpu.VMEM((bonds, width, width), BF16),
            pltpu.VMEM((bonds, width, width), BF16),
            pltpu.VMEM(left.shape, BF16),
            pltpu.VMEM(right.shape, BF16),
            pltpu.SMEM(charge.shape, jnp.int32),
            pltpu.SMEM(rank.shape, jnp.int32),
            pltpu.VMEM((rows, bonds * states, width), BF16),
            pltpu.VMEM((ITERS, states, bonds * width, width), BF16),
            pltpu.VMEM((bonds * states, bonds * states), BF16),
            pltpu.VMEM((bonds * states, 128), F32),
            pltpu.VMEM((2 * states * rows, width), F32),
            pltpu.VMEM((states, width, width), BF16),
            pltpu.VMEM((states, width, width), BF16),
            pltpu.VMEM((ITERS, 3, 8, width), F32),
            pltpu.VMEM((ITERS, nsec, 3, 8, width), F32),
            pltpu.VMEM((8, width), F32),
            pltpu.VMEM((nseg, 8, width), F32),
            pltpu.VMEM((8, width), F32),
            dma((7,)),
            dma((2,)),
            dma((CHUNKS,)),
            dma((CHUNKS, nz)),
            dma((CHUNKS, nz)),
            dma((CHUNKS, nz)),
            dma((CHUNKS, nsec)),
            dma((ITERS, nsec)),
            dma((ITERS, nsec)),
            dma((nseg,)),
            dma((nseg,)),
        ],
        compiler_params=pltpu.CompilerParams(
            collective_id=0, has_side_effects=True, vmem_limit_bytes=64 * 2**20
        ),
    )(x, env_build[0, 0], env_right[0, 0], left, right, charge, rank)
    state = (state.astype(F32) * scale).astype(BF16)
    return (state[None, None], energy.reshape(1), weight.reshape(1, 1))


def solution(mesh):
    return jax.shard_map(
        shards,
        mesh=mesh,
        in_specs=(
            P("seg", "sec", None, None, None),
            P("seg", "sec", None, None, None),
            P("seg", "sec", None, None, None),
            P(),
            P(),
            P(),
            P("sec"),
        ),
        out_specs=(P("seg", "sec", None, None, None), P("seg"), P("seg", "sec")),
        check_vma=False,
    )
```

```python
import functools

import jax
import jax.numpy as jnp
from jax import lax
from jax.experimental import pallas as pl
from jax.experimental.pallas import tpu as pltpu
from jax.sharding import PartitionSpec as P

ITERS = 2
CHUNKS = 4
MESH = pl.DeviceIdType.MESH
F32 = jnp.float32
BF16 = jnp.bfloat16


def dot(a, b):
    return jnp.dot(a, b, preferred_element_type=F32)


def iota(shape, dim):
    return lax.broadcasted_iota(jnp.int32, shape, dim)


def onehot(cond):
    return jnp.where(cond, 1.0, 0.0).astype(BF16)


def fold(values):
    return jnp.sum(values.reshape(-1, 8, values.shape[-1]), axis=0)


def whole_sum(tile):
    return jnp.sum(tile, axis=(0, 1), keepdims=True)


def order_rows(env_ref, lo, rows):
    width = env_ref.shape[2]
    lane = iota((rows, width), 1)
    blocks = []
    for first, per in ((0, 8), (8, 4)):
        parts = [env_ref[first + bond, lo : lo + rows, :].astype(F32) for bond in range(per)]
        for j in range(per):
            block = parts[0] if j == 0 else pltpu.roll(parts[0], width - j, 1)
            for bond in range(1, per):
                turned = parts[bond] if bond == j else pltpu.roll(parts[bond], (bond - j) % width, 1)
                block = jnp.where((lane & (per - 1)) == bond, turned, block)
            blocks.append(block.astype(BF16))
    return blocks


def stage_sites(site_ref, stage):
    stage[...] = jnp.zeros_like(stage)
    local = site_ref.shape[1]
    bonds = site_ref.shape[3]

    def one(bond, carry):
        for new in range(local):
            stage[pl.ds(bond * local * local + new * local, local), 0:bonds] = site_ref[bond, new].astype(F32)
        return carry

    lax.fori_loop(0, site_ref.shape[0], one, 0)


def build_mpo(left_ref, right_ref, stage):
    n = 192
    row = iota((n, 1), 0)
    tail = row >= 128
    q = jnp.where(tail, (row - 128) >> 2, row >> 3)
    bond = jnp.where(tail, 8 + (row & 3), row & 7)
    col = iota((1, n), 1)
    spread = onehot(iota((stage.shape[1], n), 0) == (iota((stage.shape[1], n), 1) >> 4))
    stage_sites(left_ref, stage)
    value = dot(stage[...].astype(BF16), spread)
    value = jnp.where((row & 3) == (col & 3), value, 0.0).astype(BF16)
    value = dot(onehot((bond == (col >> 4)) & ((q >> 2) == ((col >> 2) & 3))), value)
    left = jnp.where((q & 3) == ((col >> 2) & 3), value, 0.0).astype(BF16)
    stage_sites(right_ref, stage)
    value = dot(stage[...].astype(BF16), spread)
    value = jnp.where((row & 3) == (col & 3), value, 0.0).astype(BF16)
    value = dot(onehot(((row >> 4) == (col >> 4)) & (((row >> 2) & 3) == ((col >> 2) & 3))), value)
    right = jnp.where((row & 3) == ((col >> 2) & 3), value, 0.0).astype(BF16)
    return dot(left, right).astype(BF16)


def kernel(
    nseg, nsec,
    psi_hbm, env_hbm, renv_hbm, left_hbm, right_hbm, charge_hbm, rank_hbm,
    state_ref, scale_ref, energy_ref, weight_ref,
    l0, l1, l2, l3, own, psi_ref, env_ref, renv_ref, left_ref, right_ref, charge_ref, rank_ref, x1, x3, mpo, stage, flat, xq, acc,
    sum_tx, sum_rx, share_tx, share_rx, run,
    load_sem, out_sem, shift_sem, up_sem, down_sem, side_sem, recv_sem, sum_send, sum_recv, share_send, share_recv,
):
    seg = lax.axis_index("seg")
    sec = lax.axis_index("sec")
    nz = nsec // 2
    z = sec // 2
    core = sec % 2
    slots = (l0, l1, l2, l3)
    states, width = psi_ref.shape[0], psi_ref.shape[2]
    rows = width // CHUNKS

    pairs = (
        (env_hbm, env_ref), (psi_hbm, psi_ref), (renv_hbm, renv_ref), (left_hbm, left_ref), (right_hbm, right_ref),
        (charge_hbm, charge_ref), (rank_hbm, rank_ref),
    )
    loads = [
        pltpu.make_async_copy(src, dst, load_sem.at[i])
        for i, (src, dst) in enumerate(pairs)
    ]
    for load in loads:
        load.start()

    barrier = pltpu.get_barrier_semaphore()
    for d in range(1, nsec):
        pl.semaphore_signal(barrier, inc=1, device_id=(seg, lax.rem(sec + d, nsec)), device_id_type=MESH)
    for d in range(1, nseg):
        pl.semaphore_signal(barrier, inc=1, device_id=(lax.rem(seg + d, nseg), sec), device_id_type=MESH)

    def copy(src, dst, send, recv, to):
        return pltpu.make_async_remote_copy(
            src_ref=src, dst_ref=dst, send_sem=send, recv_sem=recv, device_id=to, device_id_type=MESH
        )

    def shift(c):
        return copy(own.at[c], slots[c].at[sec], shift_sem.at[c], recv_sem.at[c, sec], (seg + 1, sec))

    def up(c, h):
        s = sec - 2 * h
        return copy(slots[c].at[s], slots[c].at[s], up_sem.at[c, h], recv_sem.at[c, s], (seg, sec + 2))

    def down(c, h):
        s = sec + 2 * h
        return copy(slots[c].at[s], slots[c].at[s], down_sem.at[c, h], recv_sem.at[c, s], (seg, sec - 2))

    def side(c, s):
        return copy(
            slots[c].at[s], slots[c].at[s], side_sem.at[c, s // 2], recv_sem.at[c, s], (seg, sec + 1 - 2 * core)
        )

    def arrived(c, s):
        copy(slots[c].at[s], slots[c].at[s], side_sem.at[c, 0], recv_sem.at[c, s], (seg, sec)).wait_recv()

    def order(c):
        for j, block in enumerate(order_rows(env_ref, c * rows, rows)):
            own[c, :, j * width : (j + 1) * width] = block

        @pl.when(seg == 0)
        def _():
            slots[c][sec] = own[c]

    def shift_out(c):
        @pl.when(seg < nseg - 1)
        def _():
            shift(c).start()

    def hop(c, h):
        if h == 0:
            @pl.when(seg > 0)
            def _():
                arrived(c, sec)

            @pl.when(z < nz - 1)
            def _():
                up(c, 0).start()

            @pl.when(z > 0)
            def _():
                down(c, 0).start()

            side(c, sec).start()
            return

        @pl.when(z >= h)
        def _():
            arrived(c, sec - 2 * h)

            @pl.when(z < nz - 1)
            def _():
                up(c, h).start()

            side(c, sec - 2 * h).start()

        @pl.when(z + h < nz)
        def _():
            arrived(c, sec + 2 * h)

            @pl.when(z > 0)
            def _():
                down(c, h).start()

            side(c, sec + 2 * h).start()

    def settle(c):
        for k in range(nz):
            arrived(c, 2 * k + 1 - core)

    def drain():
        for c in range(CHUNKS):
            @pl.when(seg < nseg - 1)
            def _():
                shift(c).wait_send()

            for h in range(nz):
                @pl.when((z >= h) & (z < nz - 1))
                def _():
                    up(c, h).wait_send()

                @pl.when((z + h < nz) & (z > 0))
                def _():
                    down(c, h).wait_send()

                side(c, 2 * h + core).wait_send()

    def flatten(c):
        lo = pl.multiple_of(c * rows, rows)
        at = lax.rem(c, 2) * rows * states
        for p in range(states):
            flat[pl.ds(at + p, rows, stride=states), :] = psi_ref[p, pl.ds(lo, rows), :].astype(F32)

    def right_apply(c):
        at = pl.multiple_of(lax.rem(c, 2) * rows * states, rows * states)
        lhs = flat[pl.ds(at, rows * states), :].astype(BF16)
        for w in range(renv_ref.shape[0] // 2):
            rhs = jnp.concatenate([renv_ref[2 * w], renv_ref[2 * w + 1]], axis=1)
            out = dot(lhs, rhs).astype(BF16)
            for half in range(2):
                lo = (2 * w + half) * states
                x1[:, lo : lo + states, :] = out[:, half * width : (half + 1) * width].reshape(rows, states, width)

    def mpo_apply(c, turn):
        group = 16
        low = iota((states // 2, 8, width), 1) < 4

        def one(step, carry):
            operator = mpo[...]
            a = step * group
            at = pl.multiple_of(c * rows + a, group)

            def pair(j):
                out = dot(operator, jnp.concatenate([x1[a + j], x1[a + j + 8]], axis=1))
                parts = [out[:, :width], out[:, width:]]
                heads = [part[:128].reshape(states, 8, width) for part in parts]
                x3[turn, :, pl.ds(pl.multiple_of(j * width + at, 16), 16), :] = jnp.concatenate(heads, axis=1).astype(BF16)
                return [part[128:].reshape(states // 2, 8, width) for part in parts]

            for j in range(4):
                evens, odds = [], []
                for a_tail, b_tail in zip(pair(j), pair(j + 4)):
                    evens.append(jnp.where(low, a_tail, pltpu.roll(b_tail, 4, 1)))
                    odds.append(jnp.where(low, pltpu.roll(a_tail, 4, 1), b_tail))
                even = jnp.concatenate(evens, axis=1).astype(BF16)
                odd = jnp.concatenate(odds, axis=1).astype(BF16)
                both = jnp.stack([even, odd], axis=1).reshape(states, 16, width)
                x3[turn, :, pl.ds(pl.multiple_of((8 + j) * width + at, 16), 16), :] = both
            return carry

        lax.fori_loop(0, rows // group, one, 0)

    def left_of(q):
        return lax.rem(sec - charge_ref[q] + nsec, nsec)

    per = 8
    zero = jnp.zeros((8, width), F32)

    def first(half, part, keep):
        lo, some_rows = 2 * half * rows, 2 * rows

        def some(step, squares):
            for j in range(per):
                q = step * per + j
                s = left_of(q)
                h = dot(jnp.concatenate([slots[2 * half][s], slots[2 * half + 1][s]], axis=0), x3[0, q])
                u = jnp.where(keep, psi_ref[q, lo : lo + some_rows, :].astype(F32) - 0.5 * h, 0.0)
                flat[pl.ds(q, some_rows, stride=states), :] = u
                xq[q, lo : lo + some_rows, :] = u.astype(BF16)
                squares = squares + fold(u * u)
            return squares

        sum_tx[0, 0] += some(part, zero)

    def exchange(step):
        for d in range(1, nsec):
            copy(
                sum_tx.at[step], sum_rx.at[step, sec], sum_send.at[step, d], sum_recv.at[step, sec],
                (seg, lax.rem(sec + d, nsec)),
            ).start()

    def collect(step):
        for d in range(1, nsec):
            other = lax.rem(sec + d, nsec)
            copy(
                sum_tx.at[step], sum_rx.at[step, other], sum_send.at[step, d], sum_recv.at[step, other], (seg, other)
            ).wait_recv()
        total = sum_rx[step, 0]
        for other in range(1, nsec):
            total = total + sum_rx[step, other]
        return total

    loads[0].wait()
    order(0)
    pl.semaphore_wait(barrier, nsec + nseg - 2)
    shift_out(0)
    for c in range(1, CHUNKS):
        order(c)
        shift_out(c)
    for load in loads[1:]:
        load.wait()
    keep = iota((2 * rows, width), 1) < rank_ref[0]
    end = nz - 1

    def both(pair, h_lo, h_hi):
        return [(c, h) for h in range(h_lo, h_hi) for c in pair]

    before_right = {
        0: [(0, 0)],
        1: [(1, 1)],
        2: [(0, 2)],
        3: [(2, 0)],
        4: [(3, 0), (1, end)],
        5: [(2, 2)],
        6: both((2, 3), 3, end) + [(2, end), (3, end)],
    }
    before_mpo = {
        0: [(1, 0), (0, 1)],
        2: both((0, 1), 2, end)[1:],
        3: [(0, end)],
        4: [(3, 1)],
        5: [(3, 2)],
    }

    def hops(i, table):
        for k, some in table.items():
            @pl.when(i == k)
            def _():
                for c, h in some:
                    hop(c, h)

    def piece(i, carry):
        c = lax.rem(i, CHUNKS)
        hops(i, before_right)

        @pl.when(i < CHUNKS)
        def _():
            flatten(c)

        @pl.when(i == CHUNKS)
        def _():
            settle(0)
            settle(1)
            first(0, 0, keep)
            hop(2, 1)
            first(0, 1, keep)

        @pl.when(i == CHUNKS + 2)
        def _():
            settle(2)
            settle(3)
            first(1, 0, keep)
            first(1, 1, keep)
            sum_rx[0, sec] = sum_tx[0]
            exchange(0)

        right_apply(c)
        hops(i, before_mpo)

        @pl.when(i == 0)
        def _():
            mpo[...] = build_mpo(left_ref, right_ref, stage)

        mpo_apply(c, i // CHUNKS)
        return carry

    sum_tx[0] = jnp.zeros_like(sum_tx[0])
    lax.fori_loop(0, 2 * CHUNKS, piece, 0)

    count = float(nsec * states * width * width)
    total = collect(0)
    scale = lax.rsqrt(whole_sum(total[0]) / count + 1e-06)

    def result(step):
        some = pl.ds(step * per, per)
        return pltpu.make_async_copy(acc.at[some], state_ref.at[some], out_sem.at[step])

    keep_all = iota((width, width), 1) < rank_ref[0]

    def last(step, carry):
        squares, inner, own_sum = carry
        for j in range(per):
            q = step * per + j
            s = left_of(q)
            h = dot(jnp.concatenate([slot[s] for slot in slots], axis=0), x3[1, q]) * scale
            x = xq[q].astype(F32) * scale
            u = jnp.where(keep_all, x - 0.5 * h, 0.0)
            acc[q] = u.astype(BF16)
            squares = squares + fold(u * u)
            inner = inner + fold(x * h)
            own_sum = own_sum + fold(x * x)
        result(step).start()
        return squares, inner, own_sum

    sums = lax.fori_loop(0, states // per, last, (zero, zero, zero))
    sum_tx[1] = jnp.stack(sums)
    sum_rx[1, sec] = jnp.stack(sums)
    exchange(1)
    mine = whole_sum(sums[0])
    total = collect(1)
    all_squares = whole_sum(total[0])
    share = jnp.log(float(nsec) * mine / all_squares)
    share_tx[...] = jnp.broadcast_to(share, share_tx.shape)

    def share_copy(d, back):
        there = seg - d if back else seg + d
        slot = share_rx.at[there if back else seg]
        sem = share_recv.at[there if back else seg]
        return copy(share_tx, slot, share_send.at[d], sem, (there, sec))

    for d in range(1, nseg):
        @pl.when(seg + d < nseg)
        def _():
            share_copy(d, False).start()

    scale_ref[...] = lax.rsqrt(all_squares / count + 1e-06)
    energy_ref[...] = whole_sum(total[1]) / whole_sum(total[2])
    drain()
    for step in range(ITERS):
        for d in range(1, nsec):
            copy(
                sum_tx.at[step], sum_rx.at[step, sec], sum_send.at[step, d], sum_recv.at[step, sec],
                (seg, lax.rem(sec + d, nsec)),
            ).wait_send()
    for d in range(1, nseg):
        @pl.when(seg + d < nseg)
        def _():
            share_copy(d, False).wait_send()

    run[...] = share_tx[...]
    for d in range(1, nseg):
        @pl.when(seg - d >= 0)
        def _():
            share_copy(d, True).wait_recv()
            run[...] += share_rx[seg - d]

    weight_ref[...] = run[0:1, 0:1]
    for step in range(states // per):
        result(step).wait()


def shards(psi, env_build, env_right, site_left, site_right, charge, rank):
    nseg, nsec = lax.axis_size("seg"), lax.axis_size("sec")
    x = psi[0, 0]
    states, width = x.shape[0], x.shape[2]
    bonds = env_build.shape[2]
    left = site_left.transpose(0, 2, 3, 1)
    right = site_right.transpose(0, 2, 3, 1)
    hbm = pl.BlockSpec(memory_space=pltpu.HBM)
    vmem = pl.BlockSpec(memory_space=pltpu.VMEM)
    dma = pltpu.SemaphoreType.DMA
    nz = nsec // 2
    rows = width // CHUNKS
    slot = pltpu.VMEM((nsec, rows, bonds * width), BF16)
    state, scale, energy, weight = pl.pallas_call(
        functools.partial(kernel, nseg, nsec),
        out_shape=(
            jax.ShapeDtypeStruct(x.shape, BF16),
            jax.ShapeDtypeStruct((1, 1), F32),
            jax.ShapeDtypeStruct((1, 1), F32),
            jax.ShapeDtypeStruct((1, 1), F32),
        ),
        in_specs=[hbm] * 7,
        out_specs=(hbm, vmem, vmem, vmem),
        scratch_shapes=[
            slot, slot, slot, slot,
            pltpu.VMEM((CHUNKS, rows, bonds * width), BF16),
            pltpu.VMEM(x.shape, BF16),
            pltpu.VMEM((bonds, width, width), BF16),
            pltpu.VMEM((bonds, width, width), BF16),
            pltpu.VMEM(left.shape, BF16),
            pltpu.VMEM(right.shape, BF16),
            pltpu.SMEM(charge.shape, jnp.int32),
            pltpu.SMEM(rank.shape, jnp.int32),
            pltpu.VMEM((rows, bonds * states, width), BF16),
            pltpu.VMEM((ITERS, states, bonds * width, width), BF16),
            pltpu.VMEM((bonds * states, bonds * states), BF16),
            pltpu.VMEM((bonds * states, 128), F32),
            pltpu.VMEM((2 * states * rows, width), F32),
            pltpu.VMEM((states, width, width), BF16),
            pltpu.VMEM((states, width, width), BF16),
            pltpu.VMEM((ITERS, 3, 8, width), F32),
            pltpu.VMEM((ITERS, nsec, 3, 8, width), F32),
            pltpu.VMEM((8, width), F32),
            pltpu.VMEM((nseg, 8, width), F32),
            pltpu.VMEM((8, width), F32),
            dma((7,)),
            dma((2,)),
            dma((CHUNKS,)),
            dma((CHUNKS, nz)),
            dma((CHUNKS, nz)),
            dma((CHUNKS, nz)),
            dma((CHUNKS, nsec)),
            dma((ITERS, nsec)),
            dma((ITERS, nsec)),
            dma((nseg,)),
            dma((nseg,)),
        ],
        compiler_params=pltpu.CompilerParams(
            collective_id=0, has_side_effects=True, vmem_limit_bytes=64 * 2**20
        ),
    )(x, env_build[0, 0], env_right[0, 0], left, right, charge, rank)
    state = (state.astype(F32) * scale).astype(BF16)
    return (state[None, None], energy.reshape(1), weight.reshape(1, 1))


def solution(mesh):
    return jax.shard_map(
        shards,
        mesh=mesh,
        in_specs=(
            P("seg", "sec", None, None, None),
            P("seg", "sec", None, None, None),
            P("seg", "sec", None, None, None),
            P(),
            P(),
            P(),
            P("sec"),
        ),
        out_specs=(P("seg", "sec", None, None, None), P("seg"), P("seg", "sec")),
        check_vma=False,
    )
```
